128 devices in a mesh: shard: 8 (over x_lo, z), replica: 16 (over x_hi, y, core).
Axes of the slice: x: 4 (x_hi: 2, x_lo: 2; x = x_hi * 2 + x_lo), y: 4, z: 4, core: 2. Of those that a mesh axis runs over, the one named last changes fastest.
Arguments:
- tokens: bfloat16 [16, 1024, 1024], P('replica', 'shard'), may hold values from -6 to 6
- segment_ids: int32 [16, 1024], P('replica', 'shard'), may hold values from 0 to 3, as said below
- cotangent: bfloat16 [16, 1024, 1024], P('replica', 'shard'), may hold values from -6 to 6
- gain1: bfloat16 [2, 1024], P(None, 'shard'), may hold values from 0.5 to 1.5
- shift1: bfloat16 [2, 1024], P(None, 'shard'), may hold values from -1.5 to 1.5
- qkv_weight: bfloat16 [2, 1024, 3072], P(None, 'shard'), may hold values from -0.5 to 0.5
- qv_bias: bfloat16 [2, 2048], P(None, 'shard'), may hold values from -1.5 to 1.5
- out_weight: bfloat16 [2, 1024, 1024], P(None, 'shard'), may hold values from -0.75 to 0.75
- out_bias: bfloat16 [2, 1024], P(None, 'shard'), may hold values from -1.5 to 1.5
- gain2: bfloat16 [2, 1024], P(None, 'shard'), may hold values from 0.5 to 1.5
- shift2: bfloat16 [2, 1024], P(None, 'shard'), may hold values from -1.5 to 1.5
- up_weight: bfloat16 [2, 1024, 4096], P(None, 'shard'), may hold values from -0.1875 to 0.1875
- up_bias: bfloat16 [2, 4096], P(None, 'shard'), may hold values from -1.5 to 1.5
- down_weight: bfloat16 [2, 4096, 1024], P(None, 'shard'), may hold values from -0.09375 to 0.09375
- down_bias: bfloat16 [2, 1024], P(None, 'shard'), may hold values from -1.5 to 1.5
Outputs:
- output: bfloat16 [16, 1024, 1024], P('replica', 'shard')
- tokens_grad: float32 [16, 1024, 1024], P('replica', 'shard')
- gain1_grad: float32 [2, 1024], P(None, 'shard')
- shift1_grad: float32 [2, 1024], P(None, 'shard')
- qkv_weight_grad: float32 [2, 1024, 3072], P(None, 'shard')
- qv_bias_grad: float32 [2, 2048], P(None, 'shard')
- out_weight_grad: float32 [2, 1024, 1024], P(None, 'shard')
- out_bias_grad: float32 [2, 1024], P(None, 'shard')
- gain2_grad: float32 [2, 1024], P(None, 'shard')
- shift2_grad: float32 [2, 1024], P(None, 'shard')
- up_weight_grad: float32 [2, 1024, 4096], P(None, 'shard')
- up_bias_grad: float32 [2, 4096], P(None, 'shard')
- down_weight_grad: float32 [2, 4096, 1024], P(None, 'shard')
- down_bias_grad: float32 [2, 1024], P(None, 'shard')
The draws below stay inside these ranges and needn't reach their ends.
Inputs may be any that keep to these rules, and one draw needn't show every extreme that they name: `segment_ids`: along each group's 1024 tokens the ids never fall and take the values 0, 1, 2, 3 (four packed documents of uneven lengths); document 1 begins among the group's first 128 tokens and ends among its last 128.
All inputs are finite; a program needn't handle non-finite values.
Results may differ from the reference program's by a relative error of at most 0.025.
Values may be sent and summed in bfloat16 or wider, within the bound.
A program may use at most 256 MiB of HBM per device.

```python
import math
import jax
import jax.numpy as jnp
from jax import lax

D = 1024
H = 16
HD = 64
FF = 4096
LAYERS = 2
GROUPS = 16
GROUP_TOK = 1024
DEV_TOK = 128


def segment_row(key):
    first_key, second_key, third_key = jax.random.split(key, 3)
    begin = jax.random.randint(first_key, (), 1, DEV_TOK)
    finish = jax.random.randint(second_key, (), GROUP_TOK - DEV_TOK + 1, GROUP_TOK - 1)
    tail = jax.random.randint(third_key, (), finish + 1, GROUP_TOK)
    position = jnp.arange(GROUP_TOK, dtype=jnp.int32)
    return (position >= begin).astype(jnp.int32) + (position >= finish).astype(jnp.int32) + (position >= tail).astype(jnp.int32)


def draw_segment_ids(key, part):
    row_keys = jax.random.split(jax.random.fold_in(key, 7), GROUPS)
    return jax.vmap(segment_row)(row_keys)


def shared_direction(key):
    sign_bits = jax.random.randint(jax.random.fold_in(key, 101), (D,), 0, 2)
    return (2 * sign_bits - 1).astype(jnp.float32) * (1.0 / math.sqrt(D))


def clipped_normal(key, shape):
    return jnp.clip(jax.random.normal(key, shape, jnp.float32), -5.0, 5.0)


def draw_tokens(key, part):
    direction = shared_direction(key)
    key = jax.random.fold_in(key, 11)
    noise_key, sign_key, start_key = jax.random.split(key, 3)
    noise_part = clipped_normal(noise_key, (GROUPS, GROUP_TOK, D))
    span_length = max(2, GROUP_TOK * 3 // 8)
    span_start = jax.random.randint(start_key, (GROUPS, 1), 0, span_length)
    first_sign = 2 * jax.random.randint(sign_key, (GROUPS, 1), 0, 2) - 1
    position = jnp.arange(GROUP_TOK, dtype=jnp.int32)
    parity = (position[None, :] + span_start) // span_length % 2
    span_signs = (first_sign * (1 - 2 * parity)).astype(jnp.float32)
    full = noise_part + 3.0 * span_signs[:, :, None] * direction[None, None, :]
    return full.astype(jnp.bfloat16)


def draw_qkv_weight(key, part):
    direction = shared_direction(key)
    key = jax.random.fold_in(key, 13)
    noise_key, column_key = jax.random.split(key, 2)
    weight_scale = 1.0 / math.sqrt(D)
    base_part = clipped_normal(noise_key, (LAYERS, D, 3 * D)) * weight_scale
    column_signs = (2 * jax.random.randint(column_key, (D,), 0, 2) - 1).astype(jnp.float32)
    rank_part = 0.236 * direction[:, None] * column_signs[None, :]
    added = jnp.concatenate([rank_part, -rank_part, jnp.zeros((D, D), jnp.float32)], axis=1)
    return (base_part + added[None]).astype(jnp.bfloat16)


def levels(stream_key, extent, shards, low, high):
    def one(dim, parts):
        draws = jax.random.uniform(jax.random.fold_in(jax.random.fold_in(stream_key, 6), dim), (parts,), jnp.float32, low / len(shards), high / len(shards))
        return jnp.repeat(jnp.exp(draws), extent[dim] // parts).reshape((-1,) + (1,) * (len(extent) - dim - 1))

    level = one(*shards[0])
    for cut in shards[1:]:
        level = level * one(*cut)
    return level


def centred(rng, extent, spread, reach, shards=(), kind=jnp.bfloat16):
    result = jax.random.normal(rng, extent, jnp.float32) * spread
    if len(shards) > 0:
        result = levels(rng, extent, shards, -0.22, 0.18) * result
    return jnp.clip(result, min=-reach, max=reach).astype(kind)


def setup_inputs(seed: int = 0) -> dict:
    splits = jax.random.split(jax.random.key(seed), 16)
    tokens = draw_tokens(jax.random.fold_in(splits[15], 71), 0)
    segment_ids = draw_segment_ids(jax.random.fold_in(splits[15], 71), 0)
    cotangent = centred(splits[2], (GROUPS, GROUP_TOK, D), 1.0, 6.0, ((0, 16), (1, 8)))
    gain1 = jnp.clip(1.0 + 0.1 * jax.random.normal(splits[3], (LAYERS, D), jnp.float32), 0.5, 1.5).astype(jnp.bfloat16)
    shift1 = centred(splits[4], (LAYERS, D), 0.3, 1.5, ((1, 8),))
    qkv_weight = draw_qkv_weight(jax.random.fold_in(splits[15], 71), 0)
    qv_bias = centred(splits[6], (LAYERS, 2 * D), 0.3, 1.5, ((1, 8),))
    out_weight = centred(splits[7], (LAYERS, D, D), (D // 16) ** -0.5, 0.75, ((1, 8),))
    out_bias = centred(splits[8], (LAYERS, D), 0.3, 1.5, ((1, 8),))
    gain2 = jnp.clip(1.0 + 0.1 * jax.random.normal(splits[9], (LAYERS, D), jnp.float32), 0.5, 1.5).astype(jnp.bfloat16)
    shift2 = centred(splits[10], (LAYERS, D), 0.3, 1.5, ((1, 8),))
    up_weight = centred(splits[11], (LAYERS, D, FF), D ** -0.5, 0.1875, ((1, 8),))
    up_bias = centred(splits[12], (LAYERS, FF), 0.3, 1.5, ((1, 8),))
    down_weight = centred(splits[13], (LAYERS, FF, D), FF ** -0.5, 0.09375, ((1, 8),))
    down_bias = centred(splits[14], (LAYERS, D), 0.3, 1.5, ((1, 8),))
    return {"tokens": tokens, "segment_ids": segment_ids, "cotangent": cotangent, "gain1": gain1, "shift1": shift1, "qkv_weight": qkv_weight, "qv_bias": qv_bias, "out_weight": out_weight, "out_bias": out_bias, "gain2": gain2, "shift2": shift2, "up_weight": up_weight, "up_bias": up_bias, "down_weight": down_weight, "down_bias": down_bias}


@jax.custom_vjp
def low(v):
    return lax.optimization_barrier(v.astype(jnp.bfloat16)).astype(jnp.float32)

@jax.custom_vjp
def low_back(v):
    return v

def low_keep(v):
    return (low(v), None)

def low_pass(kept, grad):
    return (grad,)

def back_keep(v):
    return (v, None)

def back_low(kept, grad):
    return (low(grad),)
low.defvjp(low_keep, low_pass)
low_back.defvjp(back_keep, back_low)
highest = lax.Precision.HIGHEST

def normalize(rows, gain, shift):
    mean = lax.optimization_barrier(jnp.mean(rows, axis=-1, keepdims=True))
    centered = rows - mean
    variance = lax.optimization_barrier(jnp.mean(centered * centered, axis=-1, keepdims=True))
    return centered * lax.rsqrt(variance + 1e-05) * gain + shift

def product(left, right):
    return jnp.dot(left, right, precision=highest, preferred_element_type=jnp.float32)

def head_slopes():
    return 2.0 ** (-8.0 * (jnp.arange(H, dtype=jnp.float32) + 1.0) / H)

def attend(inputs):
    query, keys, values, segs = inputs
    position = jnp.arange(GROUP_TOK, dtype=jnp.int32)
    scores = jnp.einsum('qhd,khd->hqk', query, keys, precision=highest) * (1.0 / math.sqrt(HD))
    distance = (position[:, None] - position[None, :]).astype(jnp.float32)
    scores = low_back(scores - head_slopes()[:, None, None] * distance[None])
    allowed = (segs[:, None] == segs[None, :]) & (position[:, None] >= position[None, :])
    scores = jnp.where(allowed[None], scores, -1e+30)
    top = lax.optimization_barrier(jnp.max(scores, axis=-1, keepdims=True))
    expo = jnp.exp(scores - top)
    probs = expo / lax.optimization_barrier(jnp.sum(expo, axis=-1, keepdims=True))
    return jnp.einsum('hqk,khd->qhd', low(probs), values, precision=highest)

def heads_view(values):
    return values.reshape(GROUPS, GROUP_TOK, H, HD)

def layer(state, params, segs):
    gain_a, shift_a, w_qkv, b_qv, w_out, b_out, gain_b, shift_b, w_up, b_up, w_down, b_down = params
    hidden = low(normalize(state, gain_a, shift_a))
    bias = jnp.concatenate([b_qv[:D], jnp.zeros((D,), jnp.float32), b_qv[D:]])
    projected = low(low_back(product(hidden, w_qkv) + bias))
    query = heads_view(projected[:, :D])
    keys = heads_view(projected[:, D:2 * D])
    values = heads_view(projected[:, 2 * D:])
    mixed = lax.map(jax.checkpoint(attend), (query, keys, values, segs))
    mixed = low(low_back(mixed.reshape(GROUPS * GROUP_TOK, D)))
    middle = state + low_back(product(mixed, w_out) + b_out)
    hidden = low(normalize(middle, gain_b, shift_b))
    upped = low_back(product(hidden, w_up) + b_up)
    active = low(jax.nn.gelu(upped, approximate=True))
    return middle + low_back(product(active, w_down) + b_down)

def reference(tokens, segment_ids, cotangent, gain1, shift1, qkv_weight, qv_bias, out_weight, out_bias, gain2, shift2, up_weight, up_bias, down_weight, down_bias):
    params = [item.astype(jnp.float32) for item in (gain1, shift1, qkv_weight, qv_bias, out_weight, out_bias, gain2, shift2, up_weight, up_bias, down_weight, down_bias)]

    def forward(inputs, weights):
        state = inputs.reshape(GROUPS * GROUP_TOK, D)
        for index in range(LAYERS):
            state = layer(state, [item[index] for item in weights], segment_ids)
        return state.reshape(GROUPS, GROUP_TOK, D)
    final, pullback = jax.vjp(forward, tokens.astype(jnp.float32), params)
    inputs_grad, grads = pullback(cotangent.astype(jnp.float32))
    return (final.astype(jnp.bfloat16), inputs_grad, grads[0], grads[1], grads[2], grads[3], grads[4], grads[5], grads[6], grads[7], grads[8], grads[9], grads[10], grads[11])
```

```python
import functools
import math

import jax
import jax.numpy as jnp
from jax import lax
from jax.experimental import pallas as pl
from jax.experimental.pallas import tpu as pltpu
from jax.sharding import PartitionSpec as P

D = 1024
H = 16
HD = 64
FF = 4096
LAYERS = 2
GROUP = 1024
OWN = 128
N = 8
WQ = 3 * D // N
WU = FF // N
WA = WQ + WU
QB = 256
KC = 128
MASKED = -1e30
EPS = 1e-5
MESH = pl.DeviceIdType.MESH
F32 = jnp.float32
BF16 = jnp.bfloat16
VMEM_LIMIT = 60 * 1024 * 1024

NN = (((1,), (0,)), ((), ()))
NT = (((1,), (1,)), ((), ()))
TN = (((0,), (0,)), ((), ()))


def dot(left, right, dims=NN):
    return lax.dot_general(left, right, dims, preferred_element_type=F32)


class Place:
    def __init__(self, y_size):
        self.shard = lax.axis_index("shard")
        self.replica = lax.axis_index("replica")
        self.side, self.z = self.shard // 4, self.shard % 4
        self.chip, self.core = self.replica // 2, self.replica % 2
        self.y_size = y_size
        self.y = self.chip % y_size
        self.block = self.core * 4 + self.z
        right, left, far = (self.z + 1) % 4, (self.z + 3) % 4, (self.z + 2) % 4
        self.right = {"shard": self.side * 4 + right}
        self.left = {"shard": self.side * 4 + left}
        self.twin = {"replica": self.chip * 2 + 1 - self.core}
        mine, other = self.core * 4, (1 - self.core) * 4
        self.right_block, self.left_block, self.far_block = mine + right, mine + left, mine + far
        self.twin_block = other + self.z
        self.twin_right, self.twin_left, self.twin_far = other + right, other + left, other + far
        opposite = (1 - self.side) * 4 + self.z
        self.partner = {"shard": opposite, "replica": self.chip * 2 + 1 - self.core}
        self.needs_x = {"shard": opposite, "replica": self.chip * 2 + self.side}
        self.moves = self.core != self.side

    def at_shard(self, j):
        return {"shard": (self.shard + j) % N}

    def at_block(self, flip, j):
        core = self.core if flip == 0 else 1 - self.core
        return {"shard": (self.shard + j) % N, "replica": self.chip * 2 + core}

    def at_y(self, j):
        chip = self.chip - self.y + (self.y + j) % self.y_size
        return {"replica": chip * 2 + self.core}

    def greet(self, replicas):
        barrier = pltpu.get_barrier_semaphore()
        for i in range(N):
            for j in range(replicas):
                if i + j > 0:
                    peer = {"shard": (self.shard + i) % N, "replica": (self.replica + j) % replicas}
                    pl.semaphore_signal(barrier, inc=1, device_id=peer, device_id_type=MESH)
        pl.semaphore_wait(barrier, N * replicas - 1)


def block(index, rows=OWN, start=0):
    return pl.ds(pl.multiple_of(index * OWN + start, 16), rows)


def lanes_of(index):
    return pl.ds(pl.multiple_of(index * OWN, OWN), OWN)


class Links:
    def __init__(self, send_sems, recv_sems):
        self.send_sems, self.recv_sems, self.used = send_sems, recv_sems, 0

    def pair(self, count=1):
        index = self.used
        self.used += count
        return index

    def make(self, src, dst, peer, send, recv):
        return pltpu.make_async_remote_copy(
            src_ref=src,
            dst_ref=dst,
            send_sem=self.send_sems.at[send],
            recv_sem=self.recv_sems.at[recv],
            device_id=peer,
            device_id_type=MESH,
        )

    def copy(self, src, dst, peer):
        index = self.pair()
        copy = self.make(src, dst, peer, index, index)
        copy.start()
        return copy

    def local(self, src, dst, recv):
        pltpu.make_async_copy(src, dst, self.recv_sems.at[recv]).start()

    def landed(self, ref, recv):
        pltpu.make_async_copy(ref, ref, self.recv_sems.at[recv]).wait()

    def sent(self, ref, send):
        pltpu.make_async_copy(ref, ref, self.send_sems.at[send]).wait()


def gather(links, place, full, use):
    p = place
    half = OWN // 2

    def send(index, peer, rows=OWN, start=0):
        ref = full.at[block(index, rows, start), :]
        return links.copy(ref, ref, peer)

    low_r = send(p.block, p.right, half, 0)
    high_l = send(p.block, p.left, half, half)
    own_t = send(p.block, p.twin)
    high_r = send(p.block, p.right, half, half)
    low_l = send(p.block, p.left, half, 0)
    use(p.block)
    own_t.wait_recv()
    use(p.twin_block)
    low_r.wait_recv()
    far_low = send(p.left_block, p.right, half, 0)
    high_l.wait_recv()
    far_high = send(p.right_block, p.left, half, half)
    high_r.wait_recv()
    left_t = send(p.left_block, p.twin)
    low_l.wait_recv()
    right_t = send(p.right_block, p.twin)
    use(p.left_block)
    use(p.right_block)
    left_t.wait_recv()
    use(p.twin_left)
    right_t.wait_recv()
    use(p.twin_right)
    far_low.wait_recv()
    low_t = send(p.far_block, p.twin, half, 0)
    far_high.wait_recv()
    high_t = send(p.far_block, p.twin, half, half)
    use(p.far_block)
    low_t.wait_recv()
    high_t.wait_recv()
    use(p.twin_far)
    for copy in (low_r, high_l, own_t, high_r, low_l, far_low, far_high, left_t, right_t, low_t, high_t):
        copy.wait_send()


GATHER_COPIES = 11


def scatter(links, place, make, out, slots, beside=()):
    p = place
    half = OWN // 2
    beside = list(beside) + [lambda: None] * 2

    def rows_of(role, rows=OWN, start=0):
        return pl.ds(role * OWN + start, rows)

    def send(role, slot, peer, rows=OWN, start=0):
        return links.copy(out.at[rows_of(role, rows, start), :], slots.at[rows_of(slot, rows, start), :], peer)

    def fill(role, index):
        out[rows_of(role), :] = make(index).astype(BF16)

    def add(role, slot, rows=OWN, start=0):
        mine, theirs = rows_of(role, rows, start), rows_of(slot, rows, start)
        out[mine, :] = (out[mine, :].astype(F32) + slots[theirs, :].astype(F32)).astype(BF16)

    twins = []
    for role, index in enumerate((p.twin_far, p.twin_right, p.twin_left, p.twin_block)):
        fill(role, index)
        twins.append(send(role, role, p.twin))
    fill(4, p.far_block)
    twins[0].wait_recv()
    add(4, 0)
    far_low = send(4, 4, p.right, half, 0)
    far_high = send(4, 4, p.left, half, half)
    fill(5, p.right_block)
    twins[1].wait_recv()
    add(5, 1)
    high_r = send(5, 5, p.right, half, half)
    fill(6, p.left_block)
    twins[2].wait_recv()
    add(6, 2)
    low_l = send(6, 6, p.left, half, 0)
    own = make(p.block)
    twins[3].wait_recv()
    own = own + slots[rows_of(3), :].astype(F32)
    beside[0]()
    far_low.wait_recv()
    add(5, 4, half, 0)
    low_r = send(5, 5, p.right, half, 0)
    far_high.wait_recv()
    add(6, 4, half, half)
    high_l = send(6, 6, p.left, half, half)
    beside[1]()
    for copy in (high_r, low_l, low_r, high_l):
        copy.wait_recv()
    own = own + slots[rows_of(5), :].astype(F32) + slots[rows_of(6), :].astype(F32)
    for copy in twins + [far_low, far_high, high_r, low_l, low_r, high_l]:
        copy.wait_send()
    return own


SCATTER_COPIES = 10


def standardize(rows):
    mean = jnp.mean(rows, axis=-1, keepdims=True)
    centered = rows - mean
    variance = jnp.mean(centered * centered, axis=-1, keepdims=True)
    scale = lax.rsqrt(variance + EPS)
    return centered * scale, scale


def normalize_back(rows, gain, grad):
    unit, scale = standardize(rows)
    d_unit = grad * gain
    mean = jnp.mean(d_unit, axis=-1, keepdims=True)
    along = jnp.mean(d_unit * unit, axis=-1, keepdims=True)
    d_rows = scale * (d_unit - mean - unit * along)
    d_gain = jnp.sum(grad * unit, axis=0, keepdims=True)
    d_shift = jnp.sum(grad, axis=0, keepdims=True)
    return d_rows, d_gain, d_shift


def gelu_pair(u):
    c = math.sqrt(2.0 / math.pi)
    square = u * u
    t = jnp.tanh(c * (u + 0.044715 * u * square))
    value = 0.5 * u * (1.0 + t)
    slope = 0.5 * (1.0 + t) + 0.5 * u * (1.0 - t * t) * (c * (1.0 + 3.0 * 0.044715 * square))
    return value, slope


def head_lanes(rows, head):
    lane = lax.broadcasted_iota(jnp.int32, (1, 2 * HD), 1)
    keep = (lane // HD) == head
    return jnp.where(keep, rows, jnp.zeros_like(rows))


def masked_scores(keys, query, slope, start, chunk, block_start, edge):
    scores = dot(keys, query, NT)
    row = lax.broadcasted_iota(jnp.int32, scores.shape, 0) + chunk
    scores = scores + slope * (row - block_start).astype(F32)
    keep = row >= start
    if edge:
        col = lax.broadcasted_iota(jnp.int32, scores.shape, 1) + block_start
        keep = keep & (row <= col)
    return jnp.where(keep, scores, MASKED)


class Weights:
    def __init__(self, links, place, raw, full):
        self.links, self.p = links, place
        self.raw, self.full = raw, full
        self.rows = OWN // place.y_size
        self.first = links.pair(4)
        self.second = links.pair(4)
        self.x = links.pair(4)

    def pieces(self, kind, l, peer_shard):
        p = self.p
        rows = pl.ds(pl.multiple_of(p.y * self.rows, 16), self.rows)
        take = p.core * 4 + peer_shard % 4
        dst = self.full[kind].at[l, p.shard, p.y]
        if kind == 0:
            for part in range(3):
                cols = pl.ds(pl.multiple_of(part * D + take * OWN, OWN), OWN)
                yield self.raw[0].at[l, rows, cols], dst.at[:, part * OWN : (part + 1) * OWN]
        else:
            yield self.raw[1].at[l, rows, pl.ds(pl.multiple_of(take * WU, OWN), WU)], dst

    def start(self, kind, l):
        sem = self.first + l * 2 + kind
        for j in range(1, N):
            peer = (self.p.shard + j) % N
            for src, dst in self.pieces(kind, l, peer):
                self.links.make(src, dst, {"shard": peer}, sem, sem).start()
        for src, dst in self.pieces(kind, l, self.p.shard):
            self.links.local(src, dst, sem)

    def around(self, kind, l):
        full = self.full[kind].at[l]
        self.links.landed(full.at[:, 0], self.first + l * 2 + kind)
        sem = self.second + l * 2 + kind
        for j in range(1, self.p.y_size):
            self.links.make(full.at[:, self.p.y], full.at[:, self.p.y], self.p.at_y(j), sem, sem).start()

    def ready(self, kind, l):
        if self.p.y_size > 1:
            self.links.landed(self.full[kind].at[l, :, 0 : self.p.y_size - 1], self.second + l * 2 + kind)

    def start_x(self):
        p = self.p
        for k in (2, 3):
            sem = self.x + (k - 2) * 2
            self.links.make(self.raw[k].at[p.core], self.full[k].at[p.core], p.needs_x, sem, sem + p.core).start()

        @pl.when(jnp.logical_not(p.moves))
        def _():
            for k in (2, 3):
                for l in range(LAYERS):
                    self.links.local(self.raw[k].at[l], self.full[k].at[l], self.x + (k - 2) * 2 + l)

    def ready_x(self, kind, l):
        self.links.landed(self.full[kind].at[l], self.x + (kind - 2) * 2 + l)

    def finish(self):
        for l in range(LAYERS):
            for kind in (0, 1):
                full = self.full[kind].at[l]
                self.links.sent(full.at[0 : N - 1, 0], self.first + l * 2 + kind)
                if self.p.y_size > 1:
                    self.links.sent(full.at[:, 0 : self.p.y_size - 1], self.second + l * 2 + kind)
        for k in (2, 3):
            self.links.sent(self.full[k].at[0], self.x + (k - 2) * 2)


class Swap:
    def __init__(self, links, place, src, dst):
        self.links, self.p, self.dst = links, place, dst
        self.sem = links.pair()
        self.copy = links.make(src, dst, place.partner, self.sem, self.sem)

        @pl.when(place.moves)
        def _():
            self.copy.start()

        @pl.when(jnp.logical_not(place.moves))
        def _():
            links.local(src, dst, self.sem)

    def ready(self):
        self.links.landed(self.dst, self.sem)

    def finish(self):
        @pl.when(self.p.moves)
        def _():
            self.copy.wait_send()


REPLICAS = 16
PLANE = 16
CHIPS = 8
HALF = OWN // 2
KINDS = ("up", "down", "qkv", "out")


class Sums:
    def __init__(self, links, place, l, wide, tall, slots, totals, outs):
        self.links, self.p, self.l = links, place, l
        self.wide, self.tall = wide, tall
        self.slots, self.totals, self.outs = slots, totals, outs
        self.q = place.side * 8 + place.chip
        self.sems = links.pair(len(KINDS))
        self.give = links.pair(len(KINDS))
        self.twin = links.pair(len(KINDS))
        self.last = {}

    def part(self, kind, q):
        if kind == "up":
            return self.wide.at[self.l, block_of(q, HALF), WQ:WA]
        if kind == "qkv":
            return self.wide.at[self.l, block_of(q, HALF), 0:WQ]
        rows = WU // 8 if kind == "down" else OWN // 8
        first = OWN if kind == "down" else 0
        return self.tall.at[self.l, pl.ds(pl.multiple_of(first + (q // 2) * rows, 16), rows), half_of(q % 2)]

    def target(self, kind):
        out = self.outs[kind]
        if kind in ("up", "qkv"):
            return out.at[self.l, self.p.block, self.q % 2]
        rows = WU // 8 if kind == "down" else OWN // 8
        return out.at[self.l, block_of(self.q // 2, rows), half_of(self.q % 2)]

    def region(self, kind, core):
        out = self.outs[kind]
        return out.at[self.l, pl.ds(core * 4, 4)] if kind in ("up", "qkv") else out.at[self.l, :, half_of(core)]

    def start(self, *kinds):
        for kind in kinds:
            sem = self.sems + KINDS.index(kind)
            for j in range(1, PLANE):
                q = (self.q + j) % PLANE
                peer = {"shard": (q // 8) * 4 + self.p.z, "replica": (q % 8) * 2 + self.p.core}
                self.links.make(self.part(kind, q), self.slots[kind].at[j - 1], peer, sem, sem).start()

    def total(self, *kinds):
        for kind in kinds:
            slots = self.slots[kind]
            self.links.landed(slots, self.sems + KINDS.index(kind))
            part = self.part(kind, self.q)[...].astype(F32)
            for j in range(PLANE - 1):
                part = part + slots[j].astype(F32)
            self.totals[kind][...] = part.astype(BF16)
            sem = self.give + KINDS.index(kind)
            by_rows = kind in ("up", "qkv")
            shard = self.q // 2 if by_rows else self.p.block
            core = self.p.core if by_rows else self.q % 2
            target = self.target(kind)
            for j in range(1, CHIPS):
                peer = {"shard": shard, "replica": ((self.p.chip + j) % CHIPS) * 2 + core}
                self.links.make(self.totals[kind], target, peer, sem, sem).start()
            mine = (shard == self.p.shard) & (core == self.p.core)
            last = self.links.make(self.totals[kind], target, {"shard": shard, "replica": self.p.chip * 2 + core}, sem, sem)
            pl.when(mine)(functools.partial(self.links.local, self.totals[kind], target, sem))
            pl.when(jnp.logical_not(mine))(last.start)
            self.last[kind] = (mine, last)

    def share(self, *kinds):
        for kind in kinds:
            region = self.region(kind, self.p.core)
            self.links.landed(region, self.give + KINDS.index(kind))
            self.links.make(region, region, self.p.twin, self.twin + KINDS.index(kind), self.twin + KINDS.index(kind)).start()

    def finish(self):
        for kind in KINDS:
            index = KINDS.index(kind)
            region = self.region(kind, self.p.core)
            self.links.landed(region, self.twin + index)
            self.links.sent(region, self.twin + index)
            self.links.sent(self.slots[kind], self.sems + index)
            self.links.sent(self.slots[kind].at[0 : CHIPS - 1], self.give + index)
            mine, last = self.last[kind]
            pl.when(jnp.logical_not(mine))(last.wait_send)


def block_of(index, rows):
    return pl.ds(pl.multiple_of(index * rows, 16), rows)


def half_of(index):
    return pl.ds(pl.multiple_of(index * (D // 2), OWN), D // 2)


def part_shapes():
    return {"up": (HALF, WU), "down": (WU // 8, D // 2), "qkv": (HALF, WQ), "out": (OWN // 8, D // 2)}


class SmallSums:
    def __init__(self, links, place, mine, low, slots, total, everyone, out):
        self.links, self.p = links, place
        self.mine, self.low, self.slots, self.sum, self.everyone, self.out = mine, low, slots, total, everyone, out
        self.first, self.second = links.pair(), links.pair()

    def start(self):
        self.low[...] = self.mine[...].astype(BF16)
        for j in range(1, N):
            peer = self.p.at_shard(j)
            src = self.low.at[:, lanes_of(peer["shard"])]
            self.links.make(src, self.slots.at[j - 1], peer, self.first, self.first).start()

    def total(self):
        self.links.landed(self.slots, self.first)
        total = self.mine[:, lanes_of(self.p.shard)]
        for j in range(N - 1):
            total = total + self.slots[j].astype(F32)
        self.sum[...] = total.astype(BF16)
        for j in range(1, REPLICAS):
            peer = {"replica": (self.p.replica + j) % REPLICAS}
            self.links.make(self.sum, self.everyone.at[j - 1], peer, self.second, self.second).start()

    def finish(self):
        self.links.landed(self.everyone, self.second)
        total = self.sum[...].astype(F32)
        for j in range(REPLICAS - 1):
            total = total + self.everyone[j].astype(F32)
        self.out[...] = total
        self.links.sent(self.slots, self.first)
        self.links.sent(self.everyone, self.second)


def blocks_kernel(
    y_size,
    tokens, cotangent, raw_qkv, raw_up, raw_out, raw_down, gain1, shift1, out_bias, gain2, shift2, down_bias,
    qv_bias, up_bias, own_ids,
    output, tokens_grad, up_out, down_out, qkv_out, out_out, small_out,
    wide, tall, mine, up_slots, down_slots, qkv_slots, out_slots, up_sum, down_sum, qkv_sum, out_sum,
    small_low, small_slots, small_sum, small_every,
    w_qkv, w_up, w_out, w_down, small_wide, small, segs, small_all, segs_all, vectors, ids, starts, slopes,
    token_in, cot_in, state, hidden1, qkv, lse, mixed, middle, hidden2, act_slope, active,
    score_scr, dprob_scr, turned, mixed_turned, d_full, d_upped, branch, d_mixed, d_qkv, dk_acc, dv_acc,
    out_scr, slots, low_out, grad, send_sems, recv_sems,
):
    place = Place(y_size)
    links = Links(send_sems, recv_sems)
    own = block(place.block)
    lanes = lanes_of(place.block)
    factor = 1.0 / math.sqrt(HD)
    whole = y_size > 1
    place.greet(REPLICAS if whole else 2)

    small_wide[...] = jnp.zeros_like(small_wide)
    for l in range(LAYERS):
        for k, ref in enumerate((gain1, shift1, out_bias, gain2, shift2, down_bias)):
            small_wide[6 * l + k : 6 * l + k + 1, :] = ref[l : l + 1, :].astype(F32)
        for k in range(2):
            small_wide[12 + 2 * l + k : 13 + 2 * l + k, :] = qv_bias[l : l + 1, k * OWN : (k + 1) * OWN].astype(F32)
        for k in range(4):
            small_wide[16 + 4 * l + k : 17 + 4 * l + k, :] = up_bias[l : l + 1, k * OWN : (k + 1) * OWN].astype(F32)
    small[...] = small_wide[...].astype(BF16)
    segs[...] = jnp.broadcast_to(own_ids[...], segs.shape)
    weights = Weights(links, place, (raw_qkv, raw_up, raw_out, raw_down), (w_qkv, w_up, w_out, w_down))
    small_sem, segs_sem = links.pair(), links.pair()
    for j in range(1, N):
        links.make(small, small_all.at[place.shard], place.at_shard(j), small_sem, small_sem).start()
    links.local(small, small_all.at[place.shard], small_sem)
    swap_tokens = Swap(links, place, tokens.at[0], token_in)
    weights.start(0, 0)
    here = place.core * N + place.shard
    for flip in range(2):
        for j in range(N):
            if flip + j > 0:
                links.make(segs, segs_all.at[here], place.at_block(flip, j), segs_sem, segs_sem).start()
    links.local(segs, segs_all.at[here], segs_sem)
    links.landed(small_all, small_sem)
    for s in range(N):
        vectors[:, s * OWN : (s + 1) * OWN] = small_all[s].astype(F32)
    swap_tokens.ready()
    state[0] = token_in[...].astype(F32)
    for head in range(2):
        power = (place.block * 2 + head + 1).astype(F32) * (-8.0 / H * math.log(2.0))
        slopes[head] = jnp.exp(jnp.full((1, QB), power, F32))
    outs = dict(zip(KINDS, (up_out, down_out, qkv_out, out_out)))
    parts = dict(zip(KINDS, (up_slots, down_slots, qkv_slots, out_slots)))
    totals = dict(zip(KINDS, (up_sum, down_sum, qkv_sum, out_sum)))
    sums = [None] * LAYERS
    for l in range(LAYERS):
        if whole:
            own_parts = {k: ref.at[l] for k, ref in parts.items()}
            own_totals = {k: ref.at[l] for k, ref in totals.items()}
            sums[l] = Sums(links, place, l, wide, tall, own_parts, own_totals, outs)
    smalls = SmallSums(links, place, mine, small_low, small_slots, small_sum, small_every, small_out)
    mine[...] = jnp.zeros_like(mine)

    def vector(l, k):
        return vectors[l * 6 + k : l * 6 + k + 1, :]

    def q_or_v_bias(l, base):
        cols = lanes_of(base + place.block // 2)
        even, odd = (vectors[12 + 2 * l + k : 13 + 2 * l + k, cols] for k in range(2))
        return jnp.where(place.block % 2 == 0, even, odd)

    def weight(ref, l, cols):
        return ref[l].reshape(D, cols)

    for l in range(LAYERS):
        rows_in = state[l]
        hidden1[l, own, :] = (standardize(rows_in)[0] * vector(l, 0) + vector(l, 1)).astype(BF16)
        if l == 0:
            weights.around(0, 0)
            landing = []

            def fetch(index, landing=landing):
                landing.append(index)
        bias = jnp.concatenate([q_or_v_bias(l, 0), jnp.zeros((1, OWN), F32), q_or_v_bias(l, 4)], axis=1)

        def project(index, l=l, bias=bias):
            rows = block(index)
            qkv[l, rows, :] = (dot(hidden1[l, rows, :], weight(w_qkv, l, WQ)) + bias).astype(BF16)

        if l == 0:
            gather(links, place, hidden1.at[l], fetch)
            weights.start_x()
            weights.start(1, 0)
            weights.start(0, 1)
            weights.start(1, 1)
            swap_cot = Swap(links, place, cotangent.at[0], cot_in)
            weights.ready(0, 0)
            for index in landing:
                project(index)
            links.landed(segs_all, segs_sem)
            for s in range(N):
                ids[:, s * OWN : (s + 1) * OWN] = segs_all[place.side * N + s].astype(F32)
            row = ids[0:1, :]
            start = jnp.zeros((1, GROUP), F32)
            for value in range(3):
                count = jnp.sum(jnp.where(row == value, 1.0, 0.0), axis=1, keepdims=True)
                start = start + jnp.where(row > value, count, 0.0)
            starts[...] = start.astype(jnp.int32)
        else:
            gather(links, place, hidden1.at[l], project)

        turned[...] = qkv[l, :, 2 * OWN : 3 * OWN].T

        def attend(head, carry, l=l):
            slope = slopes[head]
            own_v = pl.ds(pl.multiple_of(head * HD, HD), HD)
            for qb in range(GROUP // QB):
                cols = slice(qb * QB, (qb + 1) * QB)
                query = head_lanes(qkv[l, cols, 0:OWN], head) * jnp.asarray(factor, BF16)
                start = starts[:, cols]
                top = jnp.full((1, QB), MASKED, F32)
                chunks = (qb + 1) * QB // KC
                for c in range(chunks):
                    keys = slice(c * KC, (c + 1) * KC)
                    edge = (c + 1) * KC > qb * QB
                    s = masked_scores(qkv[l, keys, OWN : 2 * OWN], query, slope, start, c * KC, qb * QB, edge)
                    score_scr[keys, :] = s
                    top = jnp.maximum(top, jnp.max(s, axis=0, keepdims=True))
                total = jnp.zeros((1, QB), F32)
                acc = jnp.zeros((HD, QB), F32)
                for c in range(chunks):
                    keys = slice(c * KC, (c + 1) * KC)
                    e = jnp.exp(score_scr[keys, :] - top)
                    total = total + jnp.sum(e, axis=0, keepdims=True)
                    acc = acc + dot(turned[own_v, keys], e.astype(BF16))
                mixed_turned[own_v, cols] = acc / total
                lse[l, head, :, cols] = top + jnp.log(total)
            return carry

        if l == 0:
            weights.around(1, 0)
        lax.fori_loop(0, 2, attend, 0)
        mixed[l] = mixed_turned[...].T.astype(BF16)
        weights.ready_x(2, l)
        if l == 0:
            weights.around(0, 1)
            weights.around(1, 1)

        def out_part(index, l=l):
            return dot(mixed[l, block(index), :], w_out[l])

        middle[l] = state[l] + scatter(links, place, out_part, out_scr, slots) + vector(l, 2)
        hidden2[l, own, :] = (standardize(middle[l])[0] * vector(l, 3) + vector(l, 4)).astype(BF16)
        weights.ready(1, l)
        up_bias = jnp.concatenate([vectors[16 + 4 * l + k : 17 + 4 * l + k, lanes] for k in range(4)], axis=1)

        def up(index, l=l, up_bias=up_bias):
            rows = block(index)
            value, slope = gelu_pair(dot(hidden2[l, rows, :], weight(w_up, l, WU)) + up_bias)
            active[l, rows, :] = value.astype(BF16)
            act_slope[l, rows, :] = slope

        gather(links, place, hidden2.at[l], up)
        weights.ready_x(3, l)

        def down_part(index, l=l):
            return dot(active[l, block(index), :], w_down[l])

        result = middle[l] + scatter(links, place, down_part, out_scr, slots) + vector(l, 5)
        if l + 1 < LAYERS:
            state[l + 1] = result
            weights.ready(0, l + 1)
        else:
            low_out[...] = result.astype(BF16)
    swap_output = Swap(links, place, low_out, output.at[0])
    swap_cot.ready()
    grad[...] = cot_in[...].astype(F32)

    for l in reversed(range(LAYERS)):
        d_full[own, :] = grad[...].astype(BF16)

        def down_back(index, l=l):
            rows = block(index)
            d_upped[rows, :] = (dot(d_full[rows, :], w_down[l], NT) * act_slope[l, rows, :]).astype(BF16)

        gather(links, place, d_full, down_back)
        if whole and l + 1 < LAYERS:
            sums[l + 1].total("up", "down")

        def up_back(index, l=l):
            return dot(d_upped[block(index), :], weight(w_up, l, WU), NT)

        def down_grads(l=l):
            def step(i, carry):
                cols = lanes_of(i)
                tall[l, lanes_of(1 + i), :] = dot(active[l, :, cols], d_full[...], TN).astype(BF16)
                return carry

            lax.fori_loop(0, WU // OWN, step, 0)
            mine[16 * l + 5 : 16 * l + 6, lanes] = jnp.sum(d_full[:, lanes].astype(F32), axis=0, keepdims=True)

        def up_grads(l=l):
            def step(i, carry):
                cols = lanes_of(i)
                wide[l, cols, WQ:WA] = dot(hidden2[l, :, cols], d_upped[...], TN).astype(BF16)
                return carry

            lax.fori_loop(0, D // OWN, step, 0)
            total = jnp.sum(d_upped[...].astype(F32), axis=0, keepdims=True)
            for k in range(WU // OWN):
                mine[16 * l + 6 + k : 16 * l + 7 + k, lanes] = total[:, k * OWN : (k + 1) * OWN]
            if whole:
                sums[l].start("up", "down")

        d_hidden2 = scatter(links, place, up_back, out_scr, slots, (down_grads, up_grads))
        d_rows, d_gain, d_shift = normalize_back(middle[l], vector(l, 3), d_hidden2)
        mine[16 * l + 2 : 16 * l + 3, :] = d_gain
        mine[16 * l + 3 : 16 * l + 4, :] = d_shift
        grad[...] += d_rows
        branch[own, :] = grad[...].astype(BF16)

        def out_back(index, l=l):
            rows = block(index)
            d_mixed[rows, :] = dot(branch[rows, :], w_out[l], NT).astype(BF16)

        gather(links, place, branch, out_back)
        if whole and l + 1 < LAYERS:
            sums[l + 1].total("qkv", "out")
            sums[l + 1].share("up", "down")

        turned[...] = qkv[l, :, OWN : 2 * OWN].T
        dk_acc[...] = jnp.zeros_like(dk_acc)
        dv_acc[...] = jnp.zeros_like(dv_acc)

        def attend_back(head, carry, l=l):
            slope = slopes[head]
            own_k = pl.ds(pl.multiple_of(head * HD, HD), HD)
            for qb in range(GROUP // QB):
                cols = slice(qb * QB, (qb + 1) * QB)
                query = head_lanes(qkv[l, cols, 0:OWN], head) * jnp.asarray(factor, BF16)
                d_mix = head_lanes(d_mixed[cols, :], head)
                start = starts[:, cols]
                log_total = lse[l, head, :, cols]
                delta = jnp.zeros((1, QB), F32)
                chunks = (qb + 1) * QB // KC
                for c in range(chunks):
                    keys = slice(c * KC, (c + 1) * KC)
                    edge = (c + 1) * KC > qb * QB
                    s = masked_scores(qkv[l, keys, OWN : 2 * OWN], query, slope, start, c * KC, qb * QB, edge)
                    prob = jnp.exp(s - log_total)
                    d_prob = dot(qkv[l, keys, 2 * OWN : 3 * OWN], d_mix, NT)
                    delta = delta + jnp.sum(prob * d_prob, axis=0, keepdims=True)
                    score_scr[keys, :] = prob
                    dprob_scr[keys, :] = d_prob
                    dv_acc[keys, :] += dot(prob.astype(BF16), d_mix)
                acc = jnp.zeros((HD, QB), F32)
                for c in range(chunks):
                    keys = slice(c * KC, (c + 1) * KC)
                    d_score = (score_scr[keys, :] * (dprob_scr[keys, :] - delta)).astype(BF16)
                    dk_acc[keys, :] += dot(d_score, query)
                    acc = acc + dot(turned[own_k, keys], d_score)
                mixed_turned[own_k, cols] = acc * factor
            return carry

        lax.fori_loop(0, 2, attend_back, 0)
        d_qkv[:, 0:OWN] = mixed_turned[...].T.astype(BF16)
        d_qkv[:, OWN : 2 * OWN] = dk_acc[...].astype(BF16)
        d_qkv[:, 2 * OWN : 3 * OWN] = dv_acc[...].astype(BF16)

        def qkv_back(index, l=l):
            rows = block(index)
            w = weight(w_qkv, l, WQ)
            both = dot(d_qkv[rows, 0 : 2 * OWN], w[:, 0 : 2 * OWN], NT)
            return both + dot(d_qkv[rows, 2 * OWN : 3 * OWN], w[:, 2 * OWN : 3 * OWN], NT)

        def qkv_grads(l=l):
            def step(i, carry):
                cols = lanes_of(i)
                wide[l, cols, 0:WQ] = dot(hidden1[l, :, cols], d_qkv[...], TN).astype(BF16)
                return carry

            lax.fori_loop(0, D // OWN, step, 0)

        def out_grads(l=l):
            tall[l, 0:OWN, :] = dot(mixed[l], branch[...], TN).astype(BF16)
            if whole:
                sums[l].start("qkv", "out")
            mine[16 * l + 4 : 16 * l + 5, lanes] = jnp.sum(branch[:, lanes].astype(F32), axis=0, keepdims=True)
            total = jnp.sum(d_qkv[...].astype(F32), axis=0, keepdims=True)
            for first, base in ((0, 0), (2 * OWN, 4)):
                bias = total[:, first : first + OWN]
                cols = lanes_of(base + place.block // 2)
                for k in range(2):
                    mine[16 * l + 10 + k : 16 * l + 11 + k, cols] = jnp.where(place.block % 2 == k, bias, 0.0)

        d_hidden1 = scatter(links, place, qkv_back, out_scr, slots, (qkv_grads, out_grads))
        d_rows, d_gain, d_shift = normalize_back(state[l], vector(l, 0), d_hidden1)
        mine[16 * l + 0 : 16 * l + 1, :] = d_gain
        mine[16 * l + 1 : 16 * l + 2, :] = d_shift
        grad[...] += d_rows

    swap_grad = Swap(links, place, grad, tokens_grad.at[0])
    if whole:
        smalls.start()
        sums[1].share("qkv", "out")
        sums[0].total("up", "down")
        smalls.total()
        sums[0].total("qkv", "out")
        sums[0].share("up", "down")
        smalls.finish()
        sums[0].share("qkv", "out")
    else:
        up_out[...] = wide[...]
        down_out[...] = tall[...]
        small_out[...] = mine[...]
    swap_output.ready()
    swap_grad.ready()
    weights.finish()
    links.sent(small_all.at[0 : N - 1], small_sem)
    links.sent(segs_all.at[0 : 2 * N - 1], segs_sem)
    for swap in (swap_tokens, swap_cot, swap_output, swap_grad):
        swap.finish()
    if whole:
        for layer in sums:
            layer.finish()


def in_vmem(count):
    return [pl.BlockSpec(memory_space=pltpu.VMEM)] * count


def struct(shape, dtype):
    return jax.ShapeDtypeStruct(shape, dtype)


SMALL = 32


def run_blocks(y_size, *args):
    whole = y_size > 1
    shapes = part_shapes()
    if whole:
        grads = (
            struct((LAYERS, N, 2, HALF, WU), BF16),
            struct((LAYERS, WU, D), BF16),
            struct((LAYERS, N, 2, HALF, WQ), BF16),
            struct((LAYERS, OWN, D), BF16),
            struct((SMALL, OWN), F32),
        )
    else:
        empty = struct((8, OWN), F32)
        grads = (struct((LAYERS, D, WA), BF16), struct((LAYERS, OWN + WU, D), BF16), empty, empty, struct((SMALL, D), F32))
    outs = (struct((1, OWN, D), BF16), struct((1, OWN, D), F32)) + grads
    quarter = OWN // y_size
    v = pltpu.VMEM
    scratch = [v((LAYERS, D, WA), BF16), v((LAYERS, OWN + WU, D), BF16), v((SMALL, D), F32)]
    scratch += [v((LAYERS, PLANE - 1) + shapes[kind], BF16) for kind in KINDS]
    scratch += [v((LAYERS,) + shapes[kind], BF16) for kind in KINDS]
    scratch += [
        v((SMALL, D), BF16),
        v((N - 1, SMALL, OWN), BF16),
        v((SMALL, OWN), BF16),
        v((REPLICAS - 1, SMALL, OWN), BF16),
    ]
    scratch += [
        v((LAYERS, N, y_size, quarter, WQ), BF16),
        v((LAYERS, N, y_size, quarter, WU), BF16),
        v((LAYERS, OWN, D), BF16),
        v((LAYERS, WU, D), BF16),
        v((SMALL, OWN), F32),
        v((SMALL, OWN), BF16),
        v((8, OWN), jnp.int32),
        v((N, SMALL, OWN), BF16),
        v((2 * N, 8, OWN), jnp.int32),
        v((SMALL, D), F32),
        v((8, D), F32),
        v((1, D), jnp.int32),
        v((2, 1, QB), F32),
        v((OWN, D), BF16),
        v((OWN, D), BF16),
        v((LAYERS, OWN, D), F32),
        v((LAYERS, GROUP, D), BF16),
        v((LAYERS, GROUP, WQ), BF16),
        v((LAYERS, 2, 1, GROUP), F32),
        v((LAYERS, GROUP, OWN), BF16),
        v((LAYERS, OWN, D), F32),
        v((LAYERS, GROUP, D), BF16),
        v((LAYERS, GROUP, WU), F32),
        v((LAYERS, GROUP, WU), BF16),
        v((GROUP, QB), F32),
        v((GROUP, QB), F32),
        v((OWN, GROUP), BF16),
        v((OWN, GROUP), F32),
        v((GROUP, D), BF16),
        v((GROUP, WU), BF16),
        v((GROUP, D), BF16),
        v((GROUP, OWN), BF16),
        v((GROUP, WQ), BF16),
        v((GROUP, OWN), F32),
        v((GROUP, OWN), F32),
        v((7 * OWN, D), BF16),
        v((7 * OWN, D), BF16),
        v((OWN, D), BF16),
        v((OWN, D), F32),
    ]
    copies = 4 * LAYERS * (GATHER_COPIES + SCATTER_COPIES) + 64
    return pl.pallas_call(
        functools.partial(blocks_kernel, y_size),
        out_shape=outs,
        in_specs=in_vmem(2) + [pl.BlockSpec(memory_space=pl.ANY)] * 4 + in_vmem(9),
        out_specs=in_vmem(2) + [pl.BlockSpec(memory_space=pl.ANY if whole else pltpu.VMEM)] * 4 + in_vmem(1),
        scratch_shapes=scratch + [pltpu.SemaphoreType.DMA((copies,)), pltpu.SemaphoreType.DMA((copies,))],
        compiler_params=pltpu.CompilerParams(collective_id=1, has_side_effects=True, vmem_limit_bytes=VMEM_LIMIT),
        cost_estimate=pl.CostEstimate(flops=24 << 30, bytes_accessed=32 << 20, transcendentals=16 << 20),
    )(*args)


ROWS = 32


def unpack_kernel(up, down, qkv, out, small, up_grad, down_grad, qkv_grad, out_grad,
                  g_gain1, g_shift1, g_gain2, g_shift2, g_out_bias, g_down_bias, g_qv_bias, g_up_bias):
    for l in range(LAYERS):
        here = slice(l, l + 1)
        singles = (g_gain1, g_shift1, g_gain2, g_shift2, g_out_bias, g_down_bias)
        for k, ref in enumerate(singles):
            ref[here, :] = small[16 * l + k : 16 * l + k + 1, :]
        for k in range(4):
            g_up_bias[here, k * OWN : (k + 1) * OWN] = small[16 * l + 6 + k : 16 * l + 7 + k, :]
        for k in range(2):
            g_qv_bias[here, k * OWN : (k + 1) * OWN] = small[16 * l + 10 + k : 16 * l + 11 + k, :]
    for w in range(N):
        up_grad[0, :, w * WU : (w + 1) * WU] = up[0, w, 0].astype(F32)
        for part in range(3):
            cols = slice(part * D + w * OWN, part * D + (w + 1) * OWN)
            qkv_grad[0, :, cols] = qkv[0, w, 0, :, part * OWN : (part + 1) * OWN].astype(F32)
    down_grad[0] = down[0].astype(F32)
    out_grad[0] = out[0].astype(F32)


def unpack(up, down, qkv, out, small):
    steps = OWN // ROWS
    per_half = HALF // ROWS

    def pieces(width):
        return pl.BlockSpec((1, N, 1, ROWS, width), lambda l, i: (l, 0, i // per_half, i % per_half, 0))

    def plain(rows, width):
        return pl.BlockSpec((1, rows, width), lambda l, i: (l, i, 0))

    def fixed(rows, width):
        return pl.BlockSpec((rows, width), lambda l, i: (0, 0))

    narrow = [OWN] * 6 + [2 * OWN, WU]
    return pl.pallas_call(
        unpack_kernel,
        grid=(LAYERS, steps),
        in_specs=[pieces(WU), plain(WU // steps, D), pieces(WQ), plain(ROWS, D), fixed(SMALL, OWN)],
        out_specs=[plain(ROWS, FF), plain(WU // steps, D), plain(ROWS, 3 * D), plain(ROWS, D)]
        + [fixed(LAYERS, width) for width in narrow],
        out_shape=[
            struct((LAYERS, OWN, FF), F32),
            struct((LAYERS, WU, D), F32),
            struct((LAYERS, OWN, 3 * D), F32),
            struct((LAYERS, OWN, D), F32),
        ]
        + [struct((LAYERS, width), F32) for width in narrow],
        compiler_params=pltpu.CompilerParams(vmem_limit_bytes=VMEM_LIMIT),
    )(up, down, qkv, out, small)


def per_device(y_size, reduce, tokens, segment_ids, cotangent, gain1, shift1, qkv_weight, qv_bias, out_weight, out_bias,
               gain2, shift2, up_weight, up_bias, down_weight, down_bias):
    output, grad, up, down, qkv, out, small = run_blocks(
        y_size, tokens, cotangent, qkv_weight, up_weight, out_weight, down_weight,
        gain1, shift1, out_bias, gain2, shift2, down_bias, qv_bias, up_bias, segment_ids,
    )
    if reduce is not None:
        up, down, qkv, out, small = reduce(up, down, small)
    up, down, qkv, out, g1, s1, g2, s2, ob, db, qv, ub = unpack(up, down, qkv, out, small)
    return output, grad, g1, s1, qkv, qv, out, ob, g2, s2, up, ub, down, db


def solution(mesh, reduce=None):
    rows = P(None, "shard")
    tiles = P(None, "shard", None)
    tokens = P("replica", "shard", None)
    y_size = 4 if mesh.shape["replica"] == REPLICAS else 1
    return jax.shard_map(
        functools.partial(per_device, y_size, reduce),
        mesh=mesh,
        in_specs=(
            tokens, P("replica", "shard"), tokens,
            rows, rows, tiles, rows, tiles, rows, rows, rows, tiles, rows, tiles, rows,
        ),
        out_specs=(tokens, tokens, rows, rows, tiles, rows, tiles, rows, rows, rows, tiles, rows, tiles, rows),
        check_vma=False,
    )
```

```python
import functools
import math

import jax
import jax.numpy as jnp
from jax import lax
from jax.experimental import pallas as pl
from jax.experimental.pallas import tpu as pltpu
from jax.sharding import PartitionSpec as P

D = 1024
H = 16
HD = 64
FF = 4096
LAYERS = 2
GROUP = 1024
OWN = 128
N = 8
WQ = 3 * D // N
WU = FF // N
WA = WQ + WU
QB = 256
KC = 128
MASKED = -1e30
EPS = 1e-5
MESH = pl.DeviceIdType.MESH
F32 = jnp.float32
BF16 = jnp.bfloat16
VMEM_LIMIT = 60 * 1024 * 1024

NN = (((1,), (0,)), ((), ()))
NT = (((1,), (1,)), ((), ()))
TN = (((0,), (0,)), ((), ()))


def dot(left, right, dims=NN):
    return lax.dot_general(left, right, dims, preferred_element_type=F32)


class Place:
    def __init__(self, y_size):
        self.shard = lax.axis_index("shard")
        self.replica = lax.axis_index("replica")
        self.side, self.z = self.shard // 4, self.shard % 4
        self.chip, self.core = self.replica // 2, self.replica % 2
        self.y_size = y_size
        self.y = self.chip % y_size
        self.block = self.core * 4 + self.z
        right, left, far = (self.z + 1) % 4, (self.z + 3) % 4, (self.z + 2) % 4
        self.right = {"shard": self.side * 4 + right}
        self.left = {"shard": self.side * 4 + left}
        self.twin = {"replica": self.chip * 2 + 1 - self.core}
        mine, other = self.core * 4, (1 - self.core) * 4
        self.right_block, self.left_block, self.far_block = mine + right, mine + left, mine + far
        self.twin_block = other + self.z
        self.twin_right, self.twin_left, self.twin_far = other + right, other + left, other + far
        opposite = (1 - self.side) * 4 + self.z
        self.partner = {"shard": opposite, "replica": self.chip * 2 + 1 - self.core}
        self.needs_x = {"shard": opposite, "replica": self.chip * 2 + self.side}
        self.moves = self.core != self.side

    def at_shard(self, j):
        return {"shard": (self.shard + j) % N}

    def at_block(self, flip, j):
        core = self.core if flip == 0 else 1 - self.core
        return {"shard": (self.shard + j) % N, "replica": self.chip * 2 + core}

    def at_y(self, j):
        chip = self.chip - self.y + (self.y + j) % self.y_size
        return {"replica": chip * 2 + self.core}

    def greet(self, replicas, meanwhile):
        barrier = pltpu.get_barrier_semaphore()
        for i in range(N):
            for j in range(replicas):
                if i + j > 0:
                    peer = {"shard": (self.shard + i) % N, "replica": (self.replica + j) % replicas}
                    pl.semaphore_signal(barrier, inc=1, device_id=peer, device_id_type=MESH)
        meanwhile()
        pl.semaphore_wait(barrier, N * replicas - 1)


def block(index, rows=OWN, start=0):
    return pl.ds(pl.multiple_of(index * OWN + start, 16), rows)


def lanes_of(index):
    return pl.ds(pl.multiple_of(index * OWN, OWN), OWN)


class Links:
    def __init__(self, send_sems, recv_sems):
        self.send_sems, self.recv_sems, self.used = send_sems, recv_sems, 0

    def pair(self, count=1):
        index = self.used
        self.used += count
        return index

    def make(self, src, dst, peer, send, recv):
        return pltpu.make_async_remote_copy(
            src_ref=src,
            dst_ref=dst,
            send_sem=self.send_sems.at[send],
            recv_sem=self.recv_sems.at[recv],
            device_id=peer,
            device_id_type=MESH,
        )

    def copy(self, src, dst, peer):
        index = self.pair()
        copy = self.make(src, dst, peer, index, index)
        copy.start()
        return copy

    def local(self, src, dst, recv):
        pltpu.make_async_copy(src, dst, self.recv_sems.at[recv]).start()

    def landed(self, ref, recv):
        pltpu.make_async_copy(ref, ref, self.recv_sems.at[recv]).wait()

    def sent(self, ref, send):
        pltpu.make_async_copy(ref, ref, self.send_sems.at[send]).wait()


def gather(links, place, full, use):
    p = place
    half = OWN // 2

    def send(index, peer, rows=OWN, start=0):
        ref = full.at[block(index, rows, start), :]
        return links.copy(ref, ref, peer)

    low_r = send(p.block, p.right, half, 0)
    high_l = send(p.block, p.left, half, half)
    own_t = send(p.block, p.twin)
    high_r = send(p.block, p.right, half, half)
    low_l = send(p.block, p.left, half, 0)
    use(p.block)
    own_t.wait_recv()
    use(p.twin_block)
    low_r.wait_recv()
    far_low = send(p.left_block, p.right, half, 0)
    high_l.wait_recv()
    far_high = send(p.right_block, p.left, half, half)
    high_r.wait_recv()
    left_t = send(p.left_block, p.twin)
    low_l.wait_recv()
    right_t = send(p.right_block, p.twin)
    use(p.left_block)
    use(p.right_block)
    left_t.wait_recv()
    use(p.twin_left)
    right_t.wait_recv()
    use(p.twin_right)
    far_low.wait_recv()
    low_t = send(p.far_block, p.twin, half, 0)
    far_high.wait_recv()
    high_t = send(p.far_block, p.twin, half, half)
    use(p.far_block)
    low_t.wait_recv()
    high_t.wait_recv()
    use(p.twin_far)
    for copy in (low_r, high_l, own_t, high_r, low_l, far_low, far_high, left_t, right_t, low_t, high_t):
        copy.wait_send()


GATHER_COPIES = 11


def scatter(links, place, make, out, slots, beside=()):
    p = place
    half = OWN // 2
    beside = list(beside) + [lambda: None] * 2

    def rows_of(role, rows=OWN, start=0):
        return pl.ds(role * OWN + start, rows)

    def send(role, slot, peer, rows=OWN, start=0):
        return links.copy(out.at[rows_of(role, rows, start), :], slots.at[rows_of(slot, rows, start), :], peer)

    def fill(role, index):
        out[rows_of(role), :] = make(index).astype(BF16)

    def add(role, slot, rows=OWN, start=0):
        mine, theirs = rows_of(role, rows, start), rows_of(slot, rows, start)
        out[mine, :] = (out[mine, :].astype(F32) + slots[theirs, :].astype(F32)).astype(BF16)

    twins = []
    for role, index in enumerate((p.twin_far, p.twin_right, p.twin_left, p.twin_block)):
        fill(role, index)
        twins.append(send(role, role, p.twin))
    fill(4, p.far_block)
    twins[0].wait_recv()
    add(4, 0)
    far_low = send(4, 4, p.right, half, 0)
    far_high = send(4, 4, p.left, half, half)
    fill(5, p.right_block)
    twins[1].wait_recv()
    add(5, 1)
    high_r = send(5, 5, p.right, half, half)
    fill(6, p.left_block)
    twins[2].wait_recv()
    add(6, 2)
    low_l = send(6, 6, p.left, half, 0)
    own = make(p.block)
    twins[3].wait_recv()
    own = own + slots[rows_of(3), :].astype(F32)
    beside[0]()
    far_low.wait_recv()
    add(5, 4, half, 0)
    low_r = send(5, 5, p.right, half, 0)
    far_high.wait_recv()
    add(6, 4, half, half)
    high_l = send(6, 6, p.left, half, half)
    beside[1]()
    for copy in (high_r, low_l, low_r, high_l):
        copy.wait_recv()
    own = own + slots[rows_of(5), :].astype(F32) + slots[rows_of(6), :].astype(F32)
    for copy in twins + [far_low, far_high, high_r, low_l, low_r, high_l]:
        copy.wait_send()
    return own


SCATTER_COPIES = 10


def standardize(rows):
    mean = jnp.mean(rows, axis=-1, keepdims=True)
    centered = rows - mean
    variance = jnp.mean(centered * centered, axis=-1, keepdims=True)
    scale = lax.rsqrt(variance + EPS)
    return centered * scale, scale


def normalize_back(rows, gain, grad):
    unit, scale = standardize(rows)
    d_unit = grad * gain
    mean = jnp.mean(d_unit, axis=-1, keepdims=True)
    along = jnp.mean(d_unit * unit, axis=-1, keepdims=True)
    d_rows = scale * (d_unit - mean - unit * along)
    d_gain = jnp.sum(grad * unit, axis=0, keepdims=True)
    d_shift = jnp.sum(grad, axis=0, keepdims=True)
    return d_rows, d_gain, d_shift


def gelu_pair(u):
    c = math.sqrt(2.0 / math.pi)
    square = u * u
    t = jnp.tanh(c * (u + 0.044715 * u * square))
    value = 0.5 * u * (1.0 + t)
    slope = 0.5 * (1.0 + t) + 0.5 * u * (1.0 - t * t) * (c * (1.0 + 3.0 * 0.044715 * square))
    return value, slope


def head_lanes(rows, head):
    lane = lax.broadcasted_iota(jnp.int32, (1, 2 * HD), 1)
    keep = (lane // HD) == head
    return jnp.where(keep, rows, jnp.zeros_like(rows))


def masked_scores(keys, query, slope, start, chunk, block_start, edge):
    scores = dot(keys, query, NT)
    row = lax.broadcasted_iota(jnp.int32, scores.shape, 0) + chunk
    scores = scores + slope * (row - block_start).astype(F32)
    keep = row >= start
    if edge:
        col = lax.broadcasted_iota(jnp.int32, scores.shape, 1) + block_start
        keep = keep & (row <= col)
    return jnp.where(keep, scores, MASKED)


class Weights:
    def __init__(self, links, place, raw, full):
        self.links, self.p = links, place
        self.raw, self.full = raw, full
        self.rows = OWN // place.y_size
        self.first = links.pair(4)
        self.second = links.pair(4)
        self.x = links.pair(4)

    def pieces(self, kind, l, peer_shard):
        p = self.p
        rows = pl.ds(pl.multiple_of(p.y * self.rows, 16), self.rows)
        take = p.core * 4 + peer_shard % 4
        dst = self.full[kind].at[l, p.shard, p.y]
        if kind == 0:
            for part in range(3):
                cols = pl.ds(pl.multiple_of(part * D + take * OWN, OWN), OWN)
                yield self.raw[0].at[l, rows, cols], dst.at[:, part * OWN : (part + 1) * OWN]
        else:
            yield self.raw[1].at[l, rows, pl.ds(pl.multiple_of(take * WU, OWN), WU)], dst

    def start(self, kind, l):
        sem = self.first + l * 2 + kind
        for j in range(1, N):
            peer = (self.p.shard + j) % N
            for src, dst in self.pieces(kind, l, peer):
                self.links.make(src, dst, {"shard": peer}, sem, sem).start()
        for src, dst in self.pieces(kind, l, self.p.shard):
            self.links.local(src, dst, sem)

    def around(self, kind, l):
        full = self.full[kind].at[l]
        self.links.landed(full.at[:, 0], self.first + l * 2 + kind)
        sem = self.second + l * 2 + kind
        for j in range(1, self.p.y_size):
            self.links.make(full.at[:, self.p.y], full.at[:, self.p.y], self.p.at_y(j), sem, sem).start()

    def ready(self, kind, l):
        if self.p.y_size > 1:
            self.links.landed(self.full[kind].at[l, :, 0 : self.p.y_size - 1], self.second + l * 2 + kind)

    def start_x(self):
        p = self.p
        for k in (2, 3):
            sem = self.x + (k - 2) * 2
            self.links.make(self.raw[k].at[p.core], self.full[k].at[p.core], p.needs_x, sem, sem + p.core).start()

        @pl.when(jnp.logical_not(p.moves))
        def _():
            for k in (2, 3):
                for l in range(LAYERS):
                    self.links.local(self.raw[k].at[l], self.full[k].at[l], self.x + (k - 2) * 2 + l)

    def ready_x(self, kind, l):
        self.links.landed(self.full[kind].at[l], self.x + (kind - 2) * 2 + l)

    def finish(self):
        for l in range(LAYERS):
            for kind in (0, 1):
                full = self.full[kind].at[l]
                self.links.sent(full.at[0 : N - 1, 0], self.first + l * 2 + kind)
                if self.p.y_size > 1:
                    self.links.sent(full.at[:, 0 : self.p.y_size - 1], self.second + l * 2 + kind)
        for k in (2, 3):
            self.links.sent(self.full[k].at[0], self.x + (k - 2) * 2)


class Swap:
    def __init__(self, links, place, src, dst):
        self.links, self.p, self.dst = links, place, dst
        self.sem = links.pair()
        self.copy = links.make(src, dst, place.partner, self.sem, self.sem)

        @pl.when(place.moves)
        def _():
            self.copy.start()

        @pl.when(jnp.logical_not(place.moves))
        def _():
            links.local(src, dst, self.sem)

    def ready(self):
        self.links.landed(self.dst, self.sem)

    def finish(self):
        @pl.when(self.p.moves)
        def _():
            self.copy.wait_send()


REPLICAS = 16
PLANE = 16
CHIPS = 8
HALF = OWN // 2
KINDS = ("up", "down", "qkv", "out")


class Sums:
    def __init__(self, links, place, l, wide, tall, slots, totals, outs):
        self.links, self.p, self.l = links, place, l
        self.wide, self.tall = wide, tall
        self.slots, self.totals, self.outs = slots, totals, outs
        self.q = place.side * 8 + place.chip
        self.sems = links.pair(len(KINDS))
        self.give = links.pair(len(KINDS))
        self.twin = links.pair(len(KINDS))
        self.last = {}

    def part(self, kind, q):
        if kind == "up":
            return self.wide.at[self.l, block_of(q, HALF), WQ:WA]
        if kind == "qkv":
            return self.wide.at[self.l, block_of(q, HALF), 0:WQ]
        rows = WU // 8 if kind == "down" else OWN // 8
        first = OWN if kind == "down" else 0
        return self.tall.at[self.l, pl.ds(pl.multiple_of(first + (q // 2) * rows, 16), rows), half_of(q % 2)]

    def target(self, kind):
        out = self.outs[kind]
        if kind in ("up", "qkv"):
            return out.at[self.l, self.p.block, self.q % 2]
        rows = WU // 8 if kind == "down" else OWN // 8
        return out.at[self.l, block_of(self.q // 2, rows), half_of(self.q % 2)]

    def region(self, kind, core):
        out = self.outs[kind]
        return out.at[self.l, pl.ds(core * 4, 4)] if kind in ("up", "qkv") else out.at[self.l, :, half_of(core)]

    def start(self, *kinds):
        for kind in kinds:
            sem = self.sems + KINDS.index(kind)
            for j in range(1, PLANE):
                q = (self.q + j) % PLANE
                peer = {"shard": (q // 8) * 4 + self.p.z, "replica": (q % 8) * 2 + self.p.core}
                self.links.make(self.part(kind, q), self.slots[kind].at[j - 1], peer, sem, sem).start()

    def total(self, *kinds):
        for kind in kinds:
            slots = self.slots[kind]
            self.links.landed(slots, self.sems + KINDS.index(kind))
            part = self.part(kind, self.q)[...].astype(F32)
            for j in range(PLANE - 1):
                part = part + slots[j].astype(F32)
            self.totals[kind][...] = part.astype(BF16)
            sem = self.give + KINDS.index(kind)
            by_rows = kind in ("up", "qkv")
            shard = self.q // 2 if by_rows else self.p.block
            core = self.p.core if by_rows else self.q % 2
            target = self.target(kind)
            for j in range(1, CHIPS):
                peer = {"shard": shard, "replica": ((self.p.chip + j) % CHIPS) * 2 + core}
                self.links.make(self.totals[kind], target, peer, sem, sem).start()
            mine = (shard == self.p.shard) & (core == self.p.core)
            last = self.links.make(self.totals[kind], target, {"shard": shard, "replica": self.p.chip * 2 + core}, sem, sem)
            pl.when(mine)(functools.partial(self.links.local, self.totals[kind], target, sem))
            pl.when(jnp.logical_not(mine))(last.start)
            self.last[kind] = (mine, last)

    def share(self, *kinds):
        for kind in kinds:
            region = self.region(kind, self.p.core)
            self.links.landed(region, self.give + KINDS.index(kind))
            self.links.make(region, region, self.p.twin, self.twin + KINDS.index(kind), self.twin + KINDS.index(kind)).start()

    def finish(self):
        for kind in KINDS:
            index = KINDS.index(kind)
            region = self.region(kind, self.p.core)
            self.links.landed(region, self.twin + index)
            self.links.sent(region, self.twin + index)
            self.links.sent(self.slots[kind], self.sems + index)
            self.links.sent(self.slots[kind].at[0 : CHIPS - 1], self.give + index)
            mine, last = self.last[kind]
            pl.when(jnp.logical_not(mine))(last.wait_send)


def block_of(index, rows):
    return pl.ds(pl.multiple_of(index * rows, 16), rows)


def half_of(index):
    return pl.ds(pl.multiple_of(index * (D // 2), OWN), D // 2)


def part_shapes():
    return {"up": (HALF, WU), "down": (WU // 8, D // 2), "qkv": (HALF, WQ), "out": (OWN // 8, D // 2)}


class SmallSums:
    def __init__(self, links, place, mine, low, slots, total, everyone, out):
        self.links, self.p = links, place
        self.mine, self.low, self.slots, self.sum, self.everyone, self.out = mine, low, slots, total, everyone, out
        self.first, self.second = links.pair(), links.pair()

    def start(self):
        self.low[...] = self.mine[...].astype(BF16)
        for j in range(1, N):
            peer = self.p.at_shard(j)
            src = self.low.at[:, lanes_of(peer["shard"])]
            self.links.make(src, self.slots.at[j - 1], peer, self.first, self.first).start()

    def total(self):
        self.links.landed(self.slots, self.first)
        total = self.mine[:, lanes_of(self.p.shard)]
        for j in range(N - 1):
            total = total + self.slots[j].astype(F32)
        self.sum[...] = total.astype(BF16)
        for j in range(1, REPLICAS):
            peer = {"replica": (self.p.replica + j) % REPLICAS}
            self.links.make(self.sum, self.everyone.at[j - 1], peer, self.second, self.second).start()

    def finish(self):
        self.links.landed(self.everyone, self.second)
        total = self.sum[...].astype(F32)
        for j in range(REPLICAS - 1):
            total = total + self.everyone[j].astype(F32)
        self.out[...] = total
        self.links.sent(self.slots, self.first)
        self.links.sent(self.everyone, self.second)


def blocks_kernel(
    y_size,
    tokens, cotangent, raw_qkv, raw_up, raw_out, raw_down, gain1, shift1, out_bias, gain2, shift2, down_bias,
    qv_bias, up_bias, own_ids,
    output, tokens_grad, up_out, down_out, qkv_out, out_out, small_out,
    wide, tall, mine, up_slots, down_slots, qkv_slots, out_slots, up_sum, down_sum, qkv_sum, out_sum,
    small_low, small_slots, small_sum, small_every,
    w_qkv, w_up, w_out, w_down, small_wide, small, segs, small_all, segs_all, vectors, ids, starts, slopes,
    token_in, cot_in, state, hidden1, qkv, lse, mixed, middle, hidden2, act_slope, active,
    score_scr, dprob_scr, turned, mixed_turned, d_full, d_upped, branch, d_mixed, d_qkv, dk_acc, dv_acc,
    out_scr, slots, low_out, grad, send_sems, recv_sems,
):
    place = Place(y_size)
    links = Links(send_sems, recv_sems)
    own = block(place.block)
    lanes = lanes_of(place.block)
    factor = 1.0 / math.sqrt(HD)
    whole = y_size > 1

    def pack():
        small_wide[...] = jnp.zeros_like(small_wide)
        for l in range(LAYERS):
            for k, ref in enumerate((gain1, shift1, out_bias, gain2, shift2, down_bias)):
                small_wide[6 * l + k : 6 * l + k + 1, :] = ref[l : l + 1, :].astype(F32)
            for k in range(2):
                small_wide[12 + 2 * l + k : 13 + 2 * l + k, :] = qv_bias[l : l + 1, k * OWN : (k + 1) * OWN].astype(F32)
            for k in range(4):
                small_wide[16 + 4 * l + k : 17 + 4 * l + k, :] = up_bias[l : l + 1, k * OWN : (k + 1) * OWN].astype(F32)
        small[...] = small_wide[...].astype(BF16)
        segs[...] = jnp.broadcast_to(own_ids[...], segs.shape)

    place.greet(REPLICAS if whole else 2, pack)
    weights = Weights(links, place, (raw_qkv, raw_up, raw_out, raw_down), (w_qkv, w_up, w_out, w_down))
    small_sem, segs_sem = links.pair(), links.pair()
    swap_tokens = Swap(links, place, tokens.at[0], token_in)
    for j in range(1, N):
        links.make(small, small_all.at[place.shard], place.at_shard(j), small_sem, small_sem).start()
    links.local(small, small_all.at[place.shard], small_sem)
    weights.start(0, 0)
    here = place.core * N + place.shard
    for flip in range(2):
        for j in range(N):
            if flip + j > 0:
                links.make(segs, segs_all.at[here], place.at_block(flip, j), segs_sem, segs_sem).start()
    links.local(segs, segs_all.at[here], segs_sem)
    links.landed(small_all, small_sem)
    for s in range(N):
        vectors[:, s * OWN : (s + 1) * OWN] = small_all[s].astype(F32)
    swap_tokens.ready()
    state[0] = token_in[...].astype(F32)
    for head in range(2):
        power = (place.block * 2 + head + 1).astype(F32) * (-8.0 / H * math.log(2.0))
        slopes[head] = jnp.exp(jnp.full((1, QB), power, F32))
    outs = dict(zip(KINDS, (up_out, down_out, qkv_out, out_out)))
    parts = dict(zip(KINDS, (up_slots, down_slots, qkv_slots, out_slots)))
    totals = dict(zip(KINDS, (up_sum, down_sum, qkv_sum, out_sum)))
    sums = [None] * LAYERS
    for l in range(LAYERS):
        if whole:
            own_parts = {k: ref.at[l] for k, ref in parts.items()}
            own_totals = {k: ref.at[l] for k, ref in totals.items()}
            sums[l] = Sums(links, place, l, wide, tall, own_parts, own_totals, outs)
    smalls = SmallSums(links, place, mine, small_low, small_slots, small_sum, small_every, small_out)
    mine[...] = jnp.zeros_like(mine)

    def vector(l, k):
        return vectors[l * 6 + k : l * 6 + k + 1, :]

    def q_or_v_bias(l, base):
        cols = lanes_of(base + place.block // 2)
        even, odd = (vectors[12 + 2 * l + k : 13 + 2 * l + k, cols] for k in range(2))
        return jnp.where(place.block % 2 == 0, even, odd)

    def weight(ref, l, cols):
        return ref[l].reshape(D, cols)

    for l in range(LAYERS):
        rows_in = state[l]
        hidden1[l, own, :] = (standardize(rows_in)[0] * vector(l, 0) + vector(l, 1)).astype(BF16)
        if l == 0:
            weights.around(0, 0)
            landing = []

            def fetch(index, landing=landing):
                if not landing:
                    weights.start(1, 0)
                    weights.start(0, 1)
                    weights.start(1, 1)
                    weights.start_x()
                landing.append(index)
        bias = jnp.concatenate([q_or_v_bias(l, 0), jnp.zeros((1, OWN), F32), q_or_v_bias(l, 4)], axis=1)

        def project(index, l=l, bias=bias):
            rows = block(index)
            qkv[l, rows, :] = (dot(hidden1[l, rows, :], weight(w_qkv, l, WQ)) + bias).astype(BF16)

        if l == 0:
            gather(links, place, hidden1.at[l], fetch)
            swap_cot = Swap(links, place, cotangent.at[0], cot_in)
            weights.ready(0, 0)
            for index in landing:
                project(index)
            links.landed(segs_all, segs_sem)
            for s in range(N):
                ids[:, s * OWN : (s + 1) * OWN] = segs_all[place.side * N + s].astype(F32)
            row = ids[0:1, :]
            start = jnp.zeros((1, GROUP), F32)
            for value in range(3):
                count = jnp.sum(jnp.where(row == value, 1.0, 0.0), axis=1, keepdims=True)
                start = start + jnp.where(row > value, count, 0.0)
            starts[...] = start.astype(jnp.int32)
        else:
            gather(links, place, hidden1.at[l], project)

        turned[...] = qkv[l, :, 2 * OWN : 3 * OWN].T

        def attend(head, carry, l=l):
            slope = slopes[head]
            own_v = pl.ds(pl.multiple_of(head * HD, HD), HD)
            for qb in range(GROUP // QB):
                cols = slice(qb * QB, (qb + 1) * QB)
                query = head_lanes(qkv[l, cols, 0:OWN], head) * jnp.asarray(factor, BF16)
                start = starts[:, cols]
                top = jnp.full((1, QB), MASKED, F32)
                chunks = (qb + 1) * QB // KC
                for c in range(chunks):
                    keys = slice(c * KC, (c + 1) * KC)
                    edge = (c + 1) * KC > qb * QB
                    s = masked_scores(qkv[l, keys, OWN : 2 * OWN], query, slope, start, c * KC, qb * QB, edge)
                    score_scr[keys, :] = s
                    top = jnp.maximum(top, jnp.max(s, axis=0, keepdims=True))
                total = jnp.zeros((1, QB), F32)
                acc = jnp.zeros((HD, QB), F32)
                for c in range(chunks):
                    keys = slice(c * KC, (c + 1) * KC)
                    e = jnp.exp(score_scr[keys, :] - top)
                    total = total + jnp.sum(e, axis=0, keepdims=True)
                    acc = acc + dot(turned[own_v, keys], e.astype(BF16))
                mixed_turned[own_v, cols] = acc / total
                lse[l, head, :, cols] = top + jnp.log(total)
            return carry

        if l == 0:
            weights.around(1, 0)
        lax.fori_loop(0, 2, attend, 0)
        mixed[l] = mixed_turned[...].T.astype(BF16)
        weights.ready_x(2, l)
        if l == 0:
            weights.around(0, 1)
            weights.around(1, 1)

        def out_part(index, l=l):
            return dot(mixed[l, block(index), :], w_out[l])

        middle[l] = state[l] + scatter(links, place, out_part, out_scr, slots) + vector(l, 2)
        hidden2[l, own, :] = (standardize(middle[l])[0] * vector(l, 3) + vector(l, 4)).astype(BF16)
        weights.ready(1, l)
        up_bias = jnp.concatenate([vectors[16 + 4 * l + k : 17 + 4 * l + k, lanes] for k in range(4)], axis=1)

        def up(index, l=l, up_bias=up_bias):
            rows = block(index)
            value, slope = gelu_pair(dot(hidden2[l, rows, :], weight(w_up, l, WU)) + up_bias)
            active[l, rows, :] = value.astype(BF16)
            act_slope[l, rows, :] = slope

        gather(links, place, hidden2.at[l], up)
        weights.ready_x(3, l)

        def down_part(index, l=l):
            return dot(active[l, block(index), :], w_down[l])

        result = middle[l] + scatter(links, place, down_part, out_scr, slots) + vector(l, 5)
        if l + 1 < LAYERS:
            state[l + 1] = result
            weights.ready(0, l + 1)
        else:
            low_out[...] = result.astype(BF16)
    swap_output = Swap(links, place, low_out, output.at[0])
    swap_cot.ready()
    grad[...] = cot_in[...].astype(F32)

    for l in reversed(range(LAYERS)):
        d_full[own, :] = grad[...].astype(BF16)

        def down_back(index, l=l):
            rows = block(index)
            d_upped[rows, :] = (dot(d_full[rows, :], w_down[l], NT) * act_slope[l, rows, :]).astype(BF16)

        gather(links, place, d_full, down_back)
        if whole and l + 1 < LAYERS:
            sums[l + 1].total("up", "down")

        def up_back(index, l=l):
            return dot(d_upped[block(index), :], weight(w_up, l, WU), NT)

        def down_grads(l=l):
            def step(i, carry):
                cols = lanes_of(i)
                tall[l, lanes_of(1 + i), :] = dot(active[l, :, cols], d_full[...], TN).astype(BF16)
                return carry

            lax.fori_loop(0, WU // OWN, step, 0)
            if whole:
                sums[l].start("down")
            mine[16 * l + 5 : 16 * l + 6, lanes] = jnp.sum(d_full[:, lanes].astype(F32), axis=0, keepdims=True)

        def up_grads(l=l):
            def step(i, carry):
                cols = lanes_of(i)
                wide[l, cols, WQ:WA] = dot(hidden2[l, :, cols], d_upped[...], TN).astype(BF16)
                return carry

            lax.fori_loop(0, D // OWN, step, 0)
            if whole:
                sums[l].start("up")
            total = jnp.sum(d_upped[...].astype(F32), axis=0, keepdims=True)
            for k in range(WU // OWN):
                mine[16 * l + 6 + k : 16 * l + 7 + k, lanes] = total[:, k * OWN : (k + 1) * OWN]

        d_hidden2 = scatter(links, place, up_back, out_scr, slots, (down_grads, up_grads))
        d_rows, d_gain, d_shift = normalize_back(middle[l], vector(l, 3), d_hidden2)
        mine[16 * l + 2 : 16 * l + 3, :] = d_gain
        mine[16 * l + 3 : 16 * l + 4, :] = d_shift
        grad[...] += d_rows
        branch[own, :] = grad[...].astype(BF16)

        def out_back(index, l=l):
            rows = block(index)
            d_mixed[rows, :] = dot(branch[rows, :], w_out[l], NT).astype(BF16)

        gather(links, place, branch, out_back)
        if whole and l + 1 < LAYERS:
            sums[l + 1].total("qkv", "out")
            sums[l + 1].share("up", "down")

        turned[...] = qkv[l, :, OWN : 2 * OWN].T
        dk_acc[...] = jnp.zeros_like(dk_acc)
        dv_acc[...] = jnp.zeros_like(dv_acc)

        def attend_back(head, carry, l=l):
            slope = slopes[head]
            own_k = pl.ds(pl.multiple_of(head * HD, HD), HD)
            for qb in range(GROUP // QB):
                cols = slice(qb * QB, (qb + 1) * QB)
                query = head_lanes(qkv[l, cols, 0:OWN], head) * jnp.asarray(factor, BF16)
                d_mix = head_lanes(d_mixed[cols, :], head)
                start = starts[:, cols]
                log_total = lse[l, head, :, cols]
                delta = jnp.zeros((1, QB), F32)
                chunks = (qb + 1) * QB // KC
                for c in range(chunks):
                    keys = slice(c * KC, (c + 1) * KC)
                    edge = (c + 1) * KC > qb * QB
                    s = masked_scores(qkv[l, keys, OWN : 2 * OWN], query, slope, start, c * KC, qb * QB, edge)
                    prob = jnp.exp(s - log_total)
                    d_prob = dot(qkv[l, keys, 2 * OWN : 3 * OWN], d_mix, NT)
                    delta = delta + jnp.sum(prob * d_prob, axis=0, keepdims=True)
                    score_scr[keys, :] = prob
                    dprob_scr[keys, :] = d_prob
                    dv_acc[keys, :] += dot(prob.astype(BF16), d_mix)
                acc = jnp.zeros((HD, QB), F32)
                for c in range(chunks):
                    keys = slice(c * KC, (c + 1) * KC)
                    d_score = (score_scr[keys, :] * (dprob_scr[keys, :] - delta)).astype(BF16)
                    dk_acc[keys, :] += dot(d_score, query)
                    acc = acc + dot(turned[own_k, keys], d_score)
                mixed_turned[own_k, cols] = acc * factor
            return carry

        lax.fori_loop(0, 2, attend_back, 0)
        d_qkv[:, 0:OWN] = mixed_turned[...].T.astype(BF16)
        d_qkv[:, OWN : 2 * OWN] = dk_acc[...].astype(BF16)
        d_qkv[:, 2 * OWN : 3 * OWN] = dv_acc[...].astype(BF16)

        def qkv_back(index, l=l):
            rows = block(index)
            w = weight(w_qkv, l, WQ)
            both = dot(d_qkv[rows, 0 : 2 * OWN], w[:, 0 : 2 * OWN], NT)
            return both + dot(d_qkv[rows, 2 * OWN : 3 * OWN], w[:, 2 * OWN : 3 * OWN], NT)

        def qkv_grads(l=l):
            def step(i, carry):
                cols = lanes_of(i)
                wide[l, cols, 0:WQ] = dot(hidden1[l, :, cols], d_qkv[...], TN).astype(BF16)
                return carry

            lax.fori_loop(0, D // OWN, step, 0)
            if whole:
                sums[l].start("qkv")

        def out_grads(l=l):
            tall[l, 0:OWN, :] = dot(mixed[l], branch[...], TN).astype(BF16)
            if whole:
                sums[l].start("out")
            mine[16 * l + 4 : 16 * l + 5, lanes] = jnp.sum(branch[:, lanes].astype(F32), axis=0, keepdims=True)
            total = jnp.sum(d_qkv[...].astype(F32), axis=0, keepdims=True)
            for first, base in ((0, 0), (2 * OWN, 4)):
                bias = total[:, first : first + OWN]
                cols = lanes_of(base + place.block // 2)
                for k in range(2):
                    mine[16 * l + 10 + k : 16 * l + 11 + k, cols] = jnp.where(place.block % 2 == k, bias, 0.0)

        d_hidden1 = scatter(links, place, qkv_back, out_scr, slots, (qkv_grads, out_grads))
        d_rows, d_gain, d_shift = normalize_back(state[l], vector(l, 0), d_hidden1)
        mine[16 * l + 0 : 16 * l + 1, :] = d_gain
        mine[16 * l + 1 : 16 * l + 2, :] = d_shift
        grad[...] += d_rows

    swap_grad = Swap(links, place, grad, tokens_grad.at[0])
    if whole:
        smalls.start()
        sums[1].share("qkv", "out")
        sums[0].total("up", "down")
        smalls.total()
        sums[0].total("qkv", "out")
        sums[0].share("up", "down")
        smalls.finish()
        sums[0].share("qkv", "out")
    else:
        up_out[...] = wide[...]
        down_out[...] = tall[...]
        small_out[...] = mine[...]
    swap_output.ready()
    swap_grad.ready()
    weights.finish()
    links.sent(small_all.at[0 : N - 1], small_sem)
    links.sent(segs_all.at[0 : 2 * N - 1], segs_sem)
    for swap in (swap_tokens, swap_cot, swap_output, swap_grad):
        swap.finish()
    if whole:
        for layer in sums:
            layer.finish()


def in_vmem(count):
    return [pl.BlockSpec(memory_space=pltpu.VMEM)] * count


def struct(shape, dtype):
    return jax.ShapeDtypeStruct(shape, dtype)


SMALL = 32


def run_blocks(y_size, *args):
    whole = y_size > 1
    shapes = part_shapes()
    if whole:
        grads = (
            struct((LAYERS, N, 2, HALF, WU), BF16),
            struct((LAYERS, WU, D), BF16),
            struct((LAYERS, N, 2, HALF, WQ), BF16),
            struct((LAYERS, OWN, D), BF16),
            struct((SMALL, OWN), F32),
        )
    else:
        empty = struct((8, OWN), F32)
        grads = (struct((LAYERS, D, WA), BF16), struct((LAYERS, OWN + WU, D), BF16), empty, empty, struct((SMALL, D), F32))
    outs = (struct((1, OWN, D), BF16), struct((1, OWN, D), F32)) + grads
    quarter = OWN // y_size
    v = pltpu.VMEM
    scratch = [v((LAYERS, D, WA), BF16), v((LAYERS, OWN + WU, D), BF16), v((SMALL, D), F32)]
    scratch += [v((LAYERS, PLANE - 1) + shapes[kind], BF16) for kind in KINDS]
    scratch += [v((LAYERS,) + shapes[kind], BF16) for kind in KINDS]
    scratch += [
        v((SMALL, D), BF16),
        v((N - 1, SMALL, OWN), BF16),
        v((SMALL, OWN), BF16),
        v((REPLICAS - 1, SMALL, OWN), BF16),
    ]
    scratch += [
        v((LAYERS, N, y_size, quarter, WQ), BF16),
        v((LAYERS, N, y_size, quarter, WU), BF16),
        v((LAYERS, OWN, D), BF16),
        v((LAYERS, WU, D), BF16),
        v((SMALL, OWN), F32),
        v((SMALL, OWN), BF16),
        v((8, OWN), jnp.int32),
        v((N, SMALL, OWN), BF16),
        v((2 * N, 8, OWN), jnp.int32),
        v((SMALL, D), F32),
        v((8, D), F32),
        v((1, D), jnp.int32),
        v((2, 1, QB), F32),
        v((OWN, D), BF16),
        v((OWN, D), BF16),
        v((LAYERS, OWN, D), F32),
        v((LAYERS, GROUP, D), BF16),
        v((LAYERS, GROUP, WQ), BF16),
        v((LAYERS, 2, 1, GROUP), F32),
        v((LAYERS, GROUP, OWN), BF16),
        v((LAYERS, OWN, D), F32),
        v((LAYERS, GROUP, D), BF16),
        v((LAYERS, GROUP, WU), F32),
        v((LAYERS, GROUP, WU), BF16),
        v((GROUP, QB), F32),
        v((GROUP, QB), F32),
        v((OWN, GROUP), BF16),
        v((OWN, GROUP), F32),
        v((GROUP, D), BF16),
        v((GROUP, WU), BF16),
        v((GROUP, D), BF16),
        v((GROUP, OWN), BF16),
        v((GROUP, WQ), BF16),
        v((GROUP, OWN), F32),
        v((GROUP, OWN), F32),
        v((7 * OWN, D), BF16),
        v((7 * OWN, D), BF16),
        v((OWN, D), BF16),
        v((OWN, D), F32),
    ]
    copies = 4 * LAYERS * (GATHER_COPIES + SCATTER_COPIES) + 64
    return pl.pallas_call(
        functools.partial(blocks_kernel, y_size),
        out_shape=outs,
        in_specs=in_vmem(2) + [pl.BlockSpec(memory_space=pl.ANY)] * 4 + in_vmem(9),
        out_specs=in_vmem(2) + [pl.BlockSpec(memory_space=pl.ANY if whole else pltpu.VMEM)] * 4 + in_vmem(1),
        scratch_shapes=scratch + [pltpu.SemaphoreType.DMA((copies,)), pltpu.SemaphoreType.DMA((copies,))],
        compiler_params=pltpu.CompilerParams(collective_id=1, has_side_effects=True, vmem_limit_bytes=VMEM_LIMIT),
        cost_estimate=pl.CostEstimate(flops=24 << 30, bytes_accessed=32 << 20, transcendentals=16 << 20),
    )(*args)


ROWS = 32


def unpack_kernel(up, down, qkv, out, small, up_grad, down_grad, qkv_grad, out_grad,
                  g_gain1, g_shift1, g_gain2, g_shift2, g_out_bias, g_down_bias, g_qv_bias, g_up_bias):
    for l in range(LAYERS):
        here = slice(l, l + 1)
        singles = (g_gain1, g_shift1, g_gain2, g_shift2, g_out_bias, g_down_bias)
        for k, ref in enumerate(singles):
            ref[here, :] = small[16 * l + k : 16 * l + k + 1, :]
        for k in range(4):
            g_up_bias[here, k * OWN : (k + 1) * OWN] = small[16 * l + 6 + k : 16 * l + 7 + k, :]
        for k in range(2):
            g_qv_bias[here, k * OWN : (k + 1) * OWN] = small[16 * l + 10 + k : 16 * l + 11 + k, :]
    for w in range(N):
        up_grad[0, :, w * WU : (w + 1) * WU] = up[0, w, 0].astype(F32)
        for part in range(3):
            cols = slice(part * D + w * OWN, part * D + (w + 1) * OWN)
            qkv_grad[0, :, cols] = qkv[0, w, 0, :, part * OWN : (part + 1) * OWN].astype(F32)
    down_grad[0] = down[0].astype(F32)
    out_grad[0] = out[0].astype(F32)


def unpack(up, down, qkv, out, small):
    steps = OWN // ROWS
    per_half = HALF // ROWS

    def pieces(width):
        return pl.BlockSpec((1, N, 1, ROWS, width), lambda l, i: (l, 0, i // per_half, i % per_half, 0))

    def plain(rows, width):
        return pl.BlockSpec((1, rows, width), lambda l, i: (l, i, 0))

    def fixed(rows, width):
        return pl.BlockSpec((rows, width), lambda l, i: (0, 0))

    narrow = [OWN] * 6 + [2 * OWN, WU]
    return pl.pallas_call(
        unpack_kernel,
        grid=(LAYERS, steps),
        in_specs=[pieces(WU), plain(WU // steps, D), pieces(WQ), plain(ROWS, D), fixed(SMALL, OWN)],
        out_specs=[plain(ROWS, FF), plain(WU // steps, D), plain(ROWS, 3 * D), plain(ROWS, D)]
        + [fixed(LAYERS, width) for width in narrow],
        out_shape=[
            struct((LAYERS, OWN, FF), F32),
            struct((LAYERS, WU, D), F32),
            struct((LAYERS, OWN, 3 * D), F32),
            struct((LAYERS, OWN, D), F32),
        ]
        + [struct((LAYERS, width), F32) for width in narrow],
        compiler_params=pltpu.CompilerParams(vmem_limit_bytes=VMEM_LIMIT),
    )(up, down, qkv, out, small)


def per_device(y_size, reduce, tokens, segment_ids, cotangent, gain1, shift1, qkv_weight, qv_bias, out_weight, out_bias,
               gain2, shift2, up_weight, up_bias, down_weight, down_bias):
    output, grad, up, down, qkv, out, small = run_blocks(
        y_size, tokens, cotangent, qkv_weight, up_weight, out_weight, down_weight,
        gain1, shift1, out_bias, gain2, shift2, down_bias, qv_bias, up_bias, segment_ids,
    )
    if reduce is not None:
        up, down, qkv, out, small = reduce(up, down, small)
    up, down, qkv, out, g1, s1, g2, s2, ob, db, qv, ub = unpack(up, down, qkv, out, small)
    return output, grad, g1, s1, qkv, qv, out, ob, g2, s2, up, ub, down, db


def solution(mesh, reduce=None):
    rows = P(None, "shard")
    tiles = P(None, "shard", None)
    tokens = P("replica", "shard", None)
    y_size = 4 if mesh.shape["replica"] == REPLICAS else 1
    return jax.shard_map(
        functools.partial(per_device, y_size, reduce),
        mesh=mesh,
        in_specs=(
            tokens, P("replica", "shard"), tokens,
            rows, rows, tiles, rows, tiles, rows, rows, rows, tiles, rows, tiles, rows,
        ),
        out_specs=(tokens, tokens, rows, rows, tiles, rows, tiles, rows, rows, rows, tiles, rows, tiles, rows),
        check_vma=False,
    )
```

```python
import functools
import math

import jax
import jax.numpy as jnp
from jax import lax
from jax.experimental import pallas as pl
from jax.experimental.pallas import tpu as pltpu
from jax.sharding import PartitionSpec as P

D = 1024
H = 16
HD = 64
FF = 4096
LAYERS = 2
GROUP = 1024
OWN = 128
N = 8
WQ = 3 * D // N
WU = FF // N
WA = WQ + WU
QB = 256
KC = 128
MASKED = -1e30
EPS = 1e-5
MESH = pl.DeviceIdType.MESH
F32 = jnp.float32
BF16 = jnp.bfloat16
VMEM_LIMIT = 60 * 1024 * 1024

NN = (((1,), (0,)), ((), ()))
NT = (((1,), (1,)), ((), ()))
TN = (((0,), (0,)), ((), ()))


def dot(left, right, dims=NN):
    return lax.dot_general(left, right, dims, preferred_element_type=F32)


class Place:
    def __init__(self, y_size):
        self.shard = lax.axis_index("shard")
        self.replica = lax.axis_index("replica")
        self.side, self.z = self.shard // 4, self.shard % 4
        self.chip, self.core = self.replica // 2, self.replica % 2
        self.y_size = y_size
        self.y = self.chip % y_size
        self.block = self.core * 4 + self.z
        right, left, far = (self.z + 1) % 4, (self.z + 3) % 4, (self.z + 2) % 4
        self.right = {"shard": self.side * 4 + right}
        self.left = {"shard": self.side * 4 + left}
        self.twin = {"replica": self.chip * 2 + 1 - self.core}
        mine, other = self.core * 4, (1 - self.core) * 4
        self.right_block, self.left_block, self.far_block = mine + right, mine + left, mine + far
        self.twin_block = other + self.z
        self.twin_right, self.twin_left, self.twin_far = other + right, other + left, other + far
        opposite = (1 - self.side) * 4 + self.z
        self.partner = {"shard": opposite, "replica": self.chip * 2 + 1 - self.core}
        self.needs_x = {"shard": opposite, "replica": self.chip * 2 + self.side}
        self.moves = self.core != self.side

    def at_shard(self, j):
        return {"shard": (self.shard + j) % N}

    def at_block(self, flip, j):
        core = self.core if flip == 0 else 1 - self.core
        return {"shard": (self.shard + j) % N, "replica": self.chip * 2 + core}

    def at_y(self, j):
        chip = self.chip - self.y + (self.y + j) % self.y_size
        return {"replica": chip * 2 + self.core}

    def greet(self, replicas, meanwhile):
        barrier = pltpu.get_barrier_semaphore()
        for i in range(N):
            for j in range(replicas):
                if i + j > 0:
                    peer = {"shard": (self.shard + i) % N, "replica": (self.replica + j) % replicas}
                    pl.semaphore_signal(barrier, inc=1, device_id=peer, device_id_type=MESH)
        meanwhile()
        pl.semaphore_wait(barrier, N * replicas - 1)


def block(index, rows=OWN, start=0):
    return pl.ds(pl.multiple_of(index * OWN + start, 16), rows)


def lanes_of(index):
    return pl.ds(pl.multiple_of(index * OWN, OWN), OWN)


class Links:
    def __init__(self, send_sems, recv_sems):
        self.send_sems, self.recv_sems, self.used = send_sems, recv_sems, 0

    def pair(self, count=1):
        index = self.used
        self.used += count
        return index

    def make(self, src, dst, peer, send, recv):
        return pltpu.make_async_remote_copy(
            src_ref=src,
            dst_ref=dst,
            send_sem=self.send_sems.at[send],
            recv_sem=self.recv_sems.at[recv],
            device_id=peer,
            device_id_type=MESH,
        )

    def copy(self, src, dst, peer):
        index = self.pair()
        copy = self.make(src, dst, peer, index, index)
        copy.start()
        return copy

    def local(self, src, dst, recv):
        pltpu.make_async_copy(src, dst, self.recv_sems.at[recv]).start()

    def landed(self, ref, recv):
        pltpu.make_async_copy(ref, ref, self.recv_sems.at[recv]).wait()

    def sent(self, ref, send):
        pltpu.make_async_copy(ref, ref, self.send_sems.at[send]).wait()


def gather(links, place, full, use):
    p = place
    half = OWN // 2

    def send(index, peer, rows=OWN, start=0):
        ref = full.at[block(index, rows, start), :]
        return links.copy(ref, ref, peer)

    low_r = send(p.block, p.right, half, 0)
    high_l = send(p.block, p.left, half, half)
    own_t = send(p.block, p.twin)
    high_r = send(p.block, p.right, half, half)
    low_l = send(p.block, p.left, half, 0)
    use(p.block)
    own_t.wait_recv()
    use(p.twin_block)
    low_r.wait_recv()
    far_low = send(p.left_block, p.right, half, 0)
    high_l.wait_recv()
    far_high = send(p.right_block, p.left, half, half)
    high_r.wait_recv()
    left_t = send(p.left_block, p.twin)
    low_l.wait_recv()
    right_t = send(p.right_block, p.twin)
    use(p.left_block)
    use(p.right_block)
    left_t.wait_recv()
    use(p.twin_left)
    right_t.wait_recv()
    use(p.twin_right)
    far_low.wait_recv()
    low_t = send(p.far_block, p.twin, half, 0)
    far_high.wait_recv()
    high_t = send(p.far_block, p.twin, half, half)
    use(p.far_block)
    low_t.wait_recv()
    high_t.wait_recv()
    use(p.twin_far)
    for copy in (low_r, high_l, own_t, high_r, low_l, far_low, far_high, left_t, right_t, low_t, high_t):
        copy.wait_send()


GATHER_COPIES = 11


def scatter(links, place, make, out, slots, beside=()):
    p = place
    half = OWN // 2
    beside = list(beside) + [lambda: None] * 2

    def rows_of(role, rows=OWN, start=0):
        return pl.ds(role * OWN + start, rows)

    def send(role, slot, peer, rows=OWN, start=0):
        return links.copy(out.at[rows_of(role, rows, start), :], slots.at[rows_of(slot, rows, start), :], peer)

    def fill(role, index):
        out[rows_of(role), :] = make(index).astype(BF16)

    def add(role, slot, rows=OWN, start=0):
        mine, theirs = rows_of(role, rows, start), rows_of(slot, rows, start)
        out[mine, :] = (out[mine, :].astype(F32) + slots[theirs, :].astype(F32)).astype(BF16)

    twins = []
    for role, index in enumerate((p.twin_far, p.twin_right, p.twin_left, p.twin_block)):
        fill(role, index)
        twins.append(send(role, role, p.twin))
    fill(4, p.far_block)
    twins[0].wait_recv()
    add(4, 0)
    far_low = send(4, 4, p.right, half, 0)
    far_high = send(4, 4, p.left, half, half)
    fill(5, p.right_block)
    twins[1].wait_recv()
    add(5, 1)
    high_r = send(5, 5, p.right, half, half)
    fill(6, p.left_block)
    twins[2].wait_recv()
    add(6, 2)
    low_l = send(6, 6, p.left, half, 0)
    own = make(p.block)
    twins[3].wait_recv()
    own = own + slots[rows_of(3), :].astype(F32)
    beside[0]()
    far_low.wait_recv()
    add(5, 4, half, 0)
    low_r = send(5, 5, p.right, half, 0)
    far_high.wait_recv()
    add(6, 4, half, half)
    high_l = send(6, 6, p.left, half, half)
    beside[1]()
    for copy in (high_r, low_l, low_r, high_l):
        copy.wait_recv()
    own = own + slots[rows_of(5), :].astype(F32) + slots[rows_of(6), :].astype(F32)
    for copy in twins + [far_low, far_high, high_r, low_l, low_r, high_l]:
        copy.wait_send()
    return own


SCATTER_COPIES = 10


def standardize(rows):
    mean = jnp.mean(rows, axis=-1, keepdims=True)
    centered = rows - mean
    variance = jnp.mean(centered * centered, axis=-1, keepdims=True)
    scale = lax.rsqrt(variance + EPS)
    return centered * scale, scale


def normalize_back(rows, gain, grad):
    unit, scale = standardize(rows)
    d_unit = grad * gain
    mean = jnp.mean(d_unit, axis=-1, keepdims=True)
    along = jnp.mean(d_unit * unit, axis=-1, keepdims=True)
    d_rows = scale * (d_unit - mean - unit * along)
    d_gain = jnp.sum(grad * unit, axis=0, keepdims=True)
    d_shift = jnp.sum(grad, axis=0, keepdims=True)
    return d_rows, d_gain, d_shift


def gelu_pair(u):
    c = math.sqrt(2.0 / math.pi)
    square = u * u
    t = jnp.tanh(c * (u + 0.044715 * u * square))
    value = 0.5 * u * (1.0 + t)
    slope = 0.5 * (1.0 + t) + 0.5 * u * (1.0 - t * t) * (c * (1.0 + 3.0 * 0.044715 * square))
    return value, slope


def head_lanes(rows, head):
    lane = lax.broadcasted_iota(jnp.int32, (1, 2 * HD), 1)
    keep = (lane // HD) == head
    return jnp.where(keep, rows, jnp.zeros_like(rows))


def masked_scores(keys, query, slope, start, chunk, block_start, edge):
    scores = dot(keys, query, NT)
    row = lax.broadcasted_iota(jnp.int32, scores.shape, 0) + chunk
    scores = scores + slope * (row - block_start).astype(F32)
    keep = row >= start
    if edge:
        col = lax.broadcasted_iota(jnp.int32, scores.shape, 1) + block_start
        keep = keep & (row <= col)
    return jnp.where(keep, scores, MASKED)


class Weights:
    def __init__(self, links, place, raw, full):
        self.links, self.p = links, place
        self.raw, self.full = raw, full
        self.rows = OWN // place.y_size
        self.first = links.pair(4)
        self.second = links.pair(4)
        self.x = links.pair(4)

    def pieces(self, kind, l, peer_shard):
        p = self.p
        rows = pl.ds(pl.multiple_of(p.y * self.rows, 16), self.rows)
        take = p.core * 4 + peer_shard % 4
        dst = self.full[kind].at[l, p.shard, p.y]
        if kind == 0:
            for part in range(3):
                cols = pl.ds(pl.multiple_of(part * D + take * OWN, OWN), OWN)
                yield self.raw[0].at[l, rows, cols], dst.at[:, part * OWN : (part + 1) * OWN]
        else:
            yield self.raw[1].at[l, rows, pl.ds(pl.multiple_of(take * WU, OWN), WU)], dst

    def start(self, kind, l):
        sem = self.first + l * 2 + kind
        for j in range(1, N):
            peer = (self.p.shard + j) % N
            for src, dst in self.pieces(kind, l, peer):
                self.links.make(src, dst, {"shard": peer}, sem, sem).start()
        for src, dst in self.pieces(kind, l, self.p.shard):
            self.links.local(src, dst, sem)

    def around(self, kind, l):
        full = self.full[kind].at[l]
        self.links.landed(full.at[:, 0], self.first + l * 2 + kind)
        sem = self.second + l * 2 + kind
        for j in range(1, self.p.y_size):
            self.links.make(full.at[:, self.p.y], full.at[:, self.p.y], self.p.at_y(j), sem, sem).start()

    def ready(self, kind, l):
        if self.p.y_size > 1:
            self.links.landed(self.full[kind].at[l, :, 0 : self.p.y_size - 1], self.second + l * 2 + kind)

    def start_x(self):
        p = self.p
        for k in (2, 3):
            sem = self.x + (k - 2) * 2
            self.links.make(self.raw[k].at[p.core], self.full[k].at[p.core], p.needs_x, sem, sem + p.core).start()

        @pl.when(jnp.logical_not(p.moves))
        def _():
            for k in (2, 3):
                for l in range(LAYERS):
                    self.links.local(self.raw[k].at[l], self.full[k].at[l], self.x + (k - 2) * 2 + l)

    def ready_x(self, kind, l):
        self.links.landed(self.full[kind].at[l], self.x + (kind - 2) * 2 + l)

    def finish(self):
        for l in range(LAYERS):
            for kind in (0, 1):
                full = self.full[kind].at[l]
                self.links.sent(full.at[0 : N - 1, 0], self.first + l * 2 + kind)
                if self.p.y_size > 1:
                    self.links.sent(full.at[:, 0 : self.p.y_size - 1], self.second + l * 2 + kind)
        for k in (2, 3):
            self.links.sent(self.full[k].at[0], self.x + (k - 2) * 2)


class Swap:
    def __init__(self, links, place, src, dst):
        self.links, self.p, self.dst = links, place, dst
        self.sem = links.pair()
        self.copy = links.make(src, dst, place.partner, self.sem, self.sem)

        @pl.when(place.moves)
        def _():
            self.copy.start()

        @pl.when(jnp.logical_not(place.moves))
        def _():
            links.local(src, dst, self.sem)

    def ready(self):
        self.links.landed(self.dst, self.sem)

    def finish(self):
        @pl.when(self.p.moves)
        def _():
            self.copy.wait_send()


REPLICAS = 16
CHIPS = 8
HALF = OWN // 2
KINDS = ("up", "down", "qkv", "out")


class Sums:
    def __init__(self, links, place, l, wide, tall, wholes, slots, totals, outs):
        self.links, self.p, self.l = links, place, l
        self.wide, self.tall = wide, tall
        self.wholes, self.slots, self.totals, self.outs = wholes, slots, totals, outs
        self.along_x = place.side * 2 + place.chip // 4
        self.along_y = place.chip % 4
        self.around = links.pair(len(KINDS))
        self.sems = links.pair(len(KINDS))
        self.give = links.pair(len(KINDS))
        self.twin = links.pair(len(KINDS))
        self.last = {}

    def first(self, kind):
        return self.along_x if by_rows(kind) else self.along_y

    def second(self, kind):
        return self.along_y if by_rows(kind) else self.along_x

    def number(self, kind):
        return self.first(kind) * 4 + self.second(kind)

    def at(self, x, y):
        return {"shard": (x // 2) * 4 + self.p.z, "replica": ((x % 2) * 4 + y) * 2 + self.p.core}

    def group(self, kind, first):
        if by_rows(kind):
            cols = slice(WQ, WA) if kind == "up" else slice(0, WQ)
            return self.wide.at[self.l, block_of(first, 4 * HALF), cols]
        rows = WU // 4 if kind == "down" else OWN // 4
        start = OWN if kind == "down" else 0
        return self.tall.at[self.l, pl.ds(pl.multiple_of(start + first * rows, 16), rows), :]

    def part(self, kind, q):
        if by_rows(kind):
            cols = slice(WQ, WA) if kind == "up" else slice(0, WQ)
            return self.wide.at[self.l, block_of(q, HALF), cols]
        rows = WU // 8 if kind == "down" else OWN // 8
        start = OWN if kind == "down" else 0
        return self.tall.at[self.l, pl.ds(pl.multiple_of(start + (q // 2) * rows, 16), rows), half_of(q % 2)]

    def target(self, kind):
        out, q = self.outs[kind], self.number(kind)
        if by_rows(kind):
            return out.at[self.l, self.p.block, q % 2]
        rows = WU // 8 if kind == "down" else OWN // 8
        return out.at[self.l, block_of(q // 2, rows), half_of(q % 2)]

    def region(self, kind, core):
        out = self.outs[kind]
        return out.at[self.l, pl.ds(core * 4, 4)] if by_rows(kind) else out.at[self.l, :, half_of(core)]

    def start(self, *kinds):
        for kind in kinds:
            sem = self.around + KINDS.index(kind)
            for j in range(1, 4):
                other = (self.first(kind) + j) % 4
                peer = self.at(other, self.along_y) if by_rows(kind) else self.at(self.along_x, other)
                self.links.make(self.group(kind, other), self.wholes[kind].at[j - 1], peer, sem, sem).start()

    def middle(self, *kinds):
        for kind in kinds:
            wholes = self.wholes[kind]
            self.links.landed(wholes, self.around + KINDS.index(kind))
            group = self.group(kind, self.first(kind))
            total = group[...].astype(F32)
            for j in range(3):
                total = total + wholes[j].astype(F32)
            group[...] = total.astype(BF16)
            sem = self.sems + KINDS.index(kind)
            for j in range(1, 4):
                other = (self.second(kind) + j) % 4
                peer = self.at(self.along_x, other) if by_rows(kind) else self.at(other, self.along_y)
                part = self.part(kind, self.first(kind) * 4 + other)
                self.links.make(part, self.slots[kind].at[j - 1], peer, sem, sem).start()

    def total(self, *kinds):
        for kind in kinds:
            slots, q = self.slots[kind], self.number(kind)
            self.links.landed(slots, self.sems + KINDS.index(kind))
            part = self.part(kind, q)[...].astype(F32)
            for j in range(3):
                part = part + slots[j].astype(F32)
            self.totals[kind][...] = part.astype(BF16)
            sem = self.give + KINDS.index(kind)
            shard = q // 2 if by_rows(kind) else self.p.block
            core = self.p.core if by_rows(kind) else q % 2
            target = self.target(kind)
            for j in range(1, CHIPS):
                peer = {"shard": shard, "replica": ((self.p.chip + j) % CHIPS) * 2 + core}
                self.links.make(self.totals[kind], target, peer, sem, sem).start()
            mine = (shard == self.p.shard) & (core == self.p.core)
            last = self.links.make(self.totals[kind], target, {"shard": shard, "replica": self.p.chip * 2 + core}, sem, sem)
            pl.when(mine)(functools.partial(self.links.local, self.totals[kind], target, sem))
            pl.when(jnp.logical_not(mine))(last.start)
            self.last[kind] = (mine, last)

    def share(self, *kinds):
        for kind in kinds:
            region = self.region(kind, self.p.core)
            self.links.landed(region, self.give + KINDS.index(kind))
            self.links.make(region, region, self.p.twin, self.twin + KINDS.index(kind), self.twin + KINDS.index(kind)).start()

    def finish(self):
        for kind in KINDS:
            index = KINDS.index(kind)
            region = self.region(kind, self.p.core)
            self.links.landed(region, self.twin + index)
            self.links.sent(region, self.twin + index)
            self.links.sent(self.wholes[kind], self.around + index)
            self.links.sent(self.slots[kind], self.sems + index)
            out = self.outs[kind]
            rows = (CHIPS - 1) * self.totals[kind].shape[0]
            given = out.at[self.l, 0 : CHIPS - 1, 0] if by_rows(kind) else out.at[self.l, 0:rows, 0 : D // 2]
            self.links.sent(given, self.give + index)
            mine, last = self.last[kind]
            pl.when(jnp.logical_not(mine))(last.wait_send)


def by_rows(kind):
    return kind in ("up", "qkv")


def block_of(index, rows):
    return pl.ds(pl.multiple_of(index * rows, 16), rows)


def half_of(index):
    return pl.ds(pl.multiple_of(index * (D // 2), OWN), D // 2)


def group_shapes():
    return {"up": (4 * HALF, WU), "down": (WU // 4, D), "qkv": (4 * HALF, WQ), "out": (OWN // 4, D)}


def part_shapes():
    return {"up": (HALF, WU), "down": (WU // 8, D // 2), "qkv": (HALF, WQ), "out": (OWN // 8, D // 2)}


class SmallSums:
    def __init__(self, links, place, mine, low, slots, total, everyone, out):
        self.links, self.p = links, place
        self.mine, self.low, self.slots, self.sum, self.everyone, self.out = mine, low, slots, total, everyone, out
        self.first, self.second = links.pair(), links.pair()

    def start(self):
        self.low[...] = self.mine[...].astype(BF16)
        for j in range(1, N):
            peer = self.p.at_shard(j)
            src = self.low.at[:, lanes_of(peer["shard"])]
            self.links.make(src, self.slots.at[j - 1], peer, self.first, self.first).start()

    def total(self):
        self.links.landed(self.slots, self.first)
        total = self.mine[:, lanes_of(self.p.shard)]
        for j in range(N - 1):
            total = total + self.slots[j].astype(F32)
        self.sum[...] = total.astype(BF16)
        for j in range(1, REPLICAS):
            peer = {"replica": (self.p.replica + j) % REPLICAS}
            self.links.make(self.sum, self.everyone.at[j - 1], peer, self.second, self.second).start()

    def finish(self):
        self.links.landed(self.everyone, self.second)
        total = self.sum[...].astype(F32)
        for j in range(REPLICAS - 1):
            total = total + self.everyone[j].astype(F32)
        self.out[...] = total
        self.links.sent(self.slots, self.first)
        self.links.sent(self.everyone, self.second)


def blocks_kernel(
    y_size,
    tokens, cotangent, raw_qkv, raw_up, raw_out, raw_down, gain1, shift1, out_bias, gain2, shift2, down_bias,
    qv_bias, up_bias, own_ids,
    output, tokens_grad, up_out, down_out, qkv_out, out_out, small_out,
    wide, tall, mine, up_groups, down_groups, qkv_groups, out_groups, up_slots, down_slots, qkv_slots, out_slots, up_sum, down_sum, qkv_sum, out_sum,
    small_low, small_slots, small_sum, small_every,
    w_qkv, w_up, w_out, w_down, small_wide, small, segs, small_all, segs_all, vectors, ids, starts, slopes,
    token_in, cot_in, state, hidden1, qkv, lse, mixed, middle, hidden2, act_slope, active,
    score_scr, dprob_scr, turned, mixed_turned, d_full, d_upped, branch, d_mixed, d_qkv, dk_acc, dv_acc,
    out_scr, slots, low_out, grad, send_sems, recv_sems,
):
    place = Place(y_size)
    links = Links(send_sems, recv_sems)
    own = block(place.block)
    lanes = lanes_of(place.block)
    factor = 1.0 / math.sqrt(HD)
    whole = y_size > 1

    def pack():
        small_wide[...] = jnp.zeros_like(small_wide)
        for l in range(LAYERS):
            for k, ref in enumerate((gain1, shift1, out_bias, gain2, shift2, down_bias)):
                small_wide[6 * l + k : 6 * l + k + 1, :] = ref[l : l + 1, :].astype(F32)
            for k in range(2):
                small_wide[12 + 2 * l + k : 13 + 2 * l + k, :] = qv_bias[l : l + 1, k * OWN : (k + 1) * OWN].astype(F32)
            for k in range(4):
                small_wide[16 + 4 * l + k : 17 + 4 * l + k, :] = up_bias[l : l + 1, k * OWN : (k + 1) * OWN].astype(F32)
        small[...] = small_wide[...].astype(BF16)
        segs[...] = jnp.broadcast_to(own_ids[...], segs.shape)

    place.greet(REPLICAS if whole else 2, pack)
    weights = Weights(links, place, (raw_qkv, raw_up, raw_out, raw_down), (w_qkv, w_up, w_out, w_down))
    small_sem, segs_sem = links.pair(), links.pair()
    swap_tokens = Swap(links, place, tokens.at[0], token_in)
    for j in range(1, N):
        links.make(small, small_all.at[place.shard], place.at_shard(j), small_sem, small_sem).start()
    links.local(small, small_all.at[place.shard], small_sem)
    weights.start(0, 0)
    here = place.core * N + place.shard
    for flip in range(2):
        for j in range(N):
            if flip + j > 0:
                links.make(segs, segs_all.at[here], place.at_block(flip, j), segs_sem, segs_sem).start()
    links.local(segs, segs_all.at[here], segs_sem)
    links.landed(small_all, small_sem)
    for s in range(N):
        vectors[:, s * OWN : (s + 1) * OWN] = small_all[s].astype(F32)
    swap_tokens.ready()
    state[0] = token_in[...].astype(F32)
    for head in range(2):
        power = (place.block * 2 + head + 1).astype(F32) * (-8.0 / H * math.log(2.0))
        slopes[head] = jnp.exp(jnp.full((1, QB), power, F32))
    outs = dict(zip(KINDS, (up_out, down_out, qkv_out, out_out)))
    parts = dict(zip(KINDS, (up_slots, down_slots, qkv_slots, out_slots)))
    groups = dict(zip(KINDS, (up_groups, down_groups, qkv_groups, out_groups)))
    totals = dict(zip(KINDS, (up_sum, down_sum, qkv_sum, out_sum)))
    sums = [None] * LAYERS
    for l in range(LAYERS):
        if whole:
            own_parts = {k: ref.at[l] for k, ref in parts.items()}
            own_groups = {k: ref.at[l] for k, ref in groups.items()}
            own_totals = {k: ref.at[l] for k, ref in totals.items()}
            sums[l] = Sums(links, place, l, wide, tall, own_groups, own_parts, own_totals, outs)
    smalls = SmallSums(links, place, mine, small_low, small_slots, small_sum, small_every, small_out)
    mine[...] = jnp.zeros_like(mine)

    def vector(l, k):
        return vectors[l * 6 + k : l * 6 + k + 1, :]

    def q_or_v_bias(l, base):
        cols = lanes_of(base + place.block // 2)
        even, odd = (vectors[12 + 2 * l + k : 13 + 2 * l + k, cols] for k in range(2))
        return jnp.where(place.block % 2 == 0, even, odd)

    def weight(ref, l, cols):
        return ref[l].reshape(D, cols)

    for l in range(LAYERS):
        rows_in = state[l]
        hidden1[l, own, :] = (standardize(rows_in)[0] * vector(l, 0) + vector(l, 1)).astype(BF16)
        if l == 0:
            weights.around(0, 0)
            landing = []

            def fetch(index, landing=landing):
                if not landing:
                    weights.start(1, 0)
                    weights.start(0, 1)
                    weights.start(1, 1)
                    weights.start_x()
                landing.append(index)
        bias = jnp.concatenate([q_or_v_bias(l, 0), jnp.zeros((1, OWN), F32), q_or_v_bias(l, 4)], axis=1)

        def project(index, l=l, bias=bias):
            rows = block(index)
            qkv[l, rows, :] = (dot(hidden1[l, rows, :], weight(w_qkv, l, WQ)) + bias).astype(BF16)

        if l == 0:
            gather(links, place, hidden1.at[l], fetch)
            swap_cot = Swap(links, place, cotangent.at[0], cot_in)
            weights.ready(0, 0)
            for index in landing:
                project(index)
            links.landed(segs_all, segs_sem)
            for s in range(N):
                ids[:, s * OWN : (s + 1) * OWN] = segs_all[place.side * N + s].astype(F32)
            row = ids[0:1, :]
            start = jnp.zeros((1, GROUP), F32)
            for value in range(3):
                count = jnp.sum(jnp.where(row == value, 1.0, 0.0), axis=1, keepdims=True)
                start = start + jnp.where(row > value, count, 0.0)
            starts[...] = start.astype(jnp.int32)
        else:
            gather(links, place, hidden1.at[l], project)

        turned[...] = qkv[l, :, 2 * OWN : 3 * OWN].T

        def attend(head, carry, l=l):
            slope = slopes[head]
            own_v = pl.ds(pl.multiple_of(head * HD, HD), HD)
            for qb in range(GROUP // QB):
                cols = slice(qb * QB, (qb + 1) * QB)
                query = head_lanes(qkv[l, cols, 0:OWN], head) * jnp.asarray(factor, BF16)
                start = starts[:, cols]
                top = jnp.full((1, QB), MASKED, F32)
                chunks = (qb + 1) * QB // KC
                for c in range(chunks):
                    keys = slice(c * KC, (c + 1) * KC)
                    edge = (c + 1) * KC > qb * QB
                    s = masked_scores(qkv[l, keys, OWN : 2 * OWN], query, slope, start, c * KC, qb * QB, edge)
                    score_scr[keys, :] = s
                    top = jnp.maximum(top, jnp.max(s, axis=0, keepdims=True))
                total = jnp.zeros((1, QB), F32)
                acc = jnp.zeros((HD, QB), F32)
                for c in range(chunks):
                    keys = slice(c * KC, (c + 1) * KC)
                    e = jnp.exp(score_scr[keys, :] - top)
                    total = total + jnp.sum(e, axis=0, keepdims=True)
                    acc = acc + dot(turned[own_v, keys], e.astype(BF16))
                mixed_turned[own_v, cols] = acc / total
                lse[l, head, :, cols] = top + jnp.log(total)
            return carry

        if l == 0:
            weights.around(1, 0)
        lax.fori_loop(0, 2, attend, 0)
        mixed[l] = mixed_turned[...].T.astype(BF16)
        weights.ready_x(2, l)
        if l == 0:
            weights.around(0, 1)
            weights.around(1, 1)

        def out_part(index, l=l):
            return dot(mixed[l, block(index), :], w_out[l])

        middle[l] = state[l] + scatter(links, place, out_part, out_scr, slots) + vector(l, 2)
        hidden2[l, own, :] = (standardize(middle[l])[0] * vector(l, 3) + vector(l, 4)).astype(BF16)
        weights.ready(1, l)
        up_bias = jnp.concatenate([vectors[16 + 4 * l + k : 17 + 4 * l + k, lanes] for k in range(4)], axis=1)

        def up(index, l=l, up_bias=up_bias):
            rows = block(index)
            value, slope = gelu_pair(dot(hidden2[l, rows, :], weight(w_up, l, WU)) + up_bias)
            active[l, rows, :] = value.astype(BF16)
            act_slope[l, rows, :] = slope

        gather(links, place, hidden2.at[l], up)
        weights.ready_x(3, l)

        def down_part(index, l=l):
            return dot(active[l, block(index), :], w_down[l])

        result = middle[l] + scatter(links, place, down_part, out_scr, slots) + vector(l, 5)
        if l + 1 < LAYERS:
            state[l + 1] = result
            weights.ready(0, l + 1)
        else:
            low_out[...] = result.astype(BF16)
    swap_output = Swap(links, place, low_out, output.at[0])
    swap_cot.ready()
    grad[...] = cot_in[...].astype(F32)

    for l in reversed(range(LAYERS)):
        d_full[own, :] = grad[...].astype(BF16)

        def down_back(index, l=l):
            rows = block(index)
            d_upped[rows, :] = (dot(d_full[rows, :], w_down[l], NT) * act_slope[l, rows, :]).astype(BF16)

        gather(links, place, d_full, down_back)
        if whole and l + 1 < LAYERS:
            sums[l + 1].total("down", "up")
            sums[l + 1].middle("out", "qkv")

        def up_back(index, l=l):
            return dot(d_upped[block(index), :], weight(w_up, l, WU), NT)

        def down_grads(l=l):
            def step(i, carry):
                cols = lanes_of(i)
                tall[l, lanes_of(1 + i), :] = dot(active[l, :, cols], d_full[...], TN).astype(BF16)
                return carry

            lax.fori_loop(0, WU // OWN, step, 0)
            if whole:
                sums[l].start("down")
            mine[16 * l + 5 : 16 * l + 6, lanes] = jnp.sum(d_full[:, lanes].astype(F32), axis=0, keepdims=True)

        def up_grads(l=l):
            def step(i, carry):
                cols = lanes_of(i)
                wide[l, cols, WQ:WA] = dot(hidden2[l, :, cols], d_upped[...], TN).astype(BF16)
                return carry

            lax.fori_loop(0, D // OWN, step, 0)
            if whole:
                sums[l].start("up")
            total = jnp.sum(d_upped[...].astype(F32), axis=0, keepdims=True)
            for k in range(WU // OWN):
                mine[16 * l + 6 + k : 16 * l + 7 + k, lanes] = total[:, k * OWN : (k + 1) * OWN]

        d_hidden2 = scatter(links, place, up_back, out_scr, slots, (down_grads, up_grads))
        d_rows, d_gain, d_shift = normalize_back(middle[l], vector(l, 3), d_hidden2)
        mine[16 * l + 2 : 16 * l + 3, :] = d_gain
        mine[16 * l + 3 : 16 * l + 4, :] = d_shift
        grad[...] += d_rows
        branch[own, :] = grad[...].astype(BF16)

        def out_back(index, l=l):
            rows = block(index)
            d_mixed[rows, :] = dot(branch[rows, :], w_out[l], NT).astype(BF16)

        gather(links, place, branch, out_back)
        if whole and l + 1 < LAYERS:
            sums[l + 1].total("out", "qkv")
            sums[l + 1].share("down", "up")

        turned[...] = qkv[l, :, OWN : 2 * OWN].T
        dk_acc[...] = jnp.zeros_like(dk_acc)
        dv_acc[...] = jnp.zeros_like(dv_acc)

        def attend_back(head, carry, l=l):
            slope = slopes[head]
            own_k = pl.ds(pl.multiple_of(head * HD, HD), HD)
            for qb in range(GROUP // QB):
                cols = slice(qb * QB, (qb + 1) * QB)
                query = head_lanes(qkv[l, cols, 0:OWN], head) * jnp.asarray(factor, BF16)
                d_mix = head_lanes(d_mixed[cols, :], head)
                start = starts[:, cols]
                log_total = lse[l, head, :, cols]
                delta = jnp.zeros((1, QB), F32)
                chunks = (qb + 1) * QB // KC
                for c in range(chunks):
                    keys = slice(c * KC, (c + 1) * KC)
                    edge = (c + 1) * KC > qb * QB
                    s = masked_scores(qkv[l, keys, OWN : 2 * OWN], query, slope, start, c * KC, qb * QB, edge)
                    prob = jnp.exp(s - log_total)
                    d_prob = dot(qkv[l, keys, 2 * OWN : 3 * OWN], d_mix, NT)
                    delta = delta + jnp.sum(prob * d_prob, axis=0, keepdims=True)
                    score_scr[keys, :] = prob
                    dprob_scr[keys, :] = d_prob
                    dv_acc[keys, :] += dot(prob.astype(BF16), d_mix)
                acc = jnp.zeros((HD, QB), F32)
                for c in range(chunks):
                    keys = slice(c * KC, (c + 1) * KC)
                    d_score = (score_scr[keys, :] * (dprob_scr[keys, :] - delta)).astype(BF16)
                    dk_acc[keys, :] += dot(d_score, query)
                    acc = acc + dot(turned[own_k, keys], d_score)
                mixed_turned[own_k, cols] = acc * factor
            return carry

        lax.fori_loop(0, 2, attend_back, 0)
        if whole:
            sums[l].middle("down", "up")
            if l + 1 < LAYERS:
                sums[l + 1].share("out", "qkv")
        d_qkv[:, 0:OWN] = mixed_turned[...].T.astype(BF16)
        d_qkv[:, OWN : 2 * OWN] = dk_acc[...].astype(BF16)
        d_qkv[:, 2 * OWN : 3 * OWN] = dv_acc[...].astype(BF16)

        def qkv_back(index, l=l):
            rows = block(index)
            w = weight(w_qkv, l, WQ)
            both = dot(d_qkv[rows, 0 : 2 * OWN], w[:, 0 : 2 * OWN], NT)
            return both + dot(d_qkv[rows, 2 * OWN : 3 * OWN], w[:, 2 * OWN : 3 * OWN], NT)

        def qkv_grads(l=l):
            def step(i, carry):
                cols = lanes_of(i)
                wide[l, cols, 0:WQ] = dot(hidden1[l, :, cols], d_qkv[...], TN).astype(BF16)
                return carry

            lax.fori_loop(0, D // OWN, step, 0)
            if whole:
                sums[l].start("qkv")

        def out_grads(l=l):
            tall[l, 0:OWN, :] = dot(mixed[l], branch[...], TN).astype(BF16)
            if whole:
                sums[l].start("out")
                if l == 0:
                    sums[l].total("down", "up")
            mine[16 * l + 4 : 16 * l + 5, lanes] = jnp.sum(branch[:, lanes].astype(F32), axis=0, keepdims=True)
            total = jnp.sum(d_qkv[...].astype(F32), axis=0, keepdims=True)
            for first, base in ((0, 0), (2 * OWN, 4)):
                bias = total[:, first : first + OWN]
                cols = lanes_of(base + place.block // 2)
                for k in range(2):
                    mine[16 * l + 10 + k : 16 * l + 11 + k, cols] = jnp.where(place.block % 2 == k, bias, 0.0)

        d_hidden1 = scatter(links, place, qkv_back, out_scr, slots, (qkv_grads, out_grads))
        d_rows, d_gain, d_shift = normalize_back(state[l], vector(l, 0), d_hidden1)
        mine[16 * l + 0 : 16 * l + 1, :] = d_gain
        mine[16 * l + 1 : 16 * l + 2, :] = d_shift
        grad[...] += d_rows

    swap_grad = Swap(links, place, grad, tokens_grad.at[0])
    if whole:
        smalls.start()
        sums[0].middle("out", "qkv")
        smalls.total()
        sums[0].total("out", "qkv")
        sums[0].share("down", "up")
        smalls.finish()
        sums[0].share("out", "qkv")
    else:
        up_out[...] = wide[...]
        down_out[...] = tall[...]
        small_out[...] = mine[...]
    swap_output.ready()
    swap_grad.ready()
    weights.finish()
    links.sent(small_all.at[0 : N - 1], small_sem)
    links.sent(segs_all.at[0 : 2 * N - 1], segs_sem)
    for swap in (swap_tokens, swap_cot, swap_output, swap_grad):
        swap.finish()
    if whole:
        for layer in sums:
            layer.finish()


def in_vmem(count):
    return [pl.BlockSpec(memory_space=pltpu.VMEM)] * count


def struct(shape, dtype):
    return jax.ShapeDtypeStruct(shape, dtype)


SMALL = 32


def run_blocks(y_size, *args):
    whole = y_size > 1
    shapes = part_shapes()
    if whole:
        grads = (
            struct((LAYERS, N, 2, HALF, WU), BF16),
            struct((LAYERS, WU, D), BF16),
            struct((LAYERS, N, 2, HALF, WQ), BF16),
            struct((LAYERS, OWN, D), BF16),
            struct((SMALL, OWN), F32),
        )
    else:
        empty = struct((8, OWN), F32)
        grads = (struct((LAYERS, D, WA), BF16), struct((LAYERS, OWN + WU, D), BF16), empty, empty, struct((SMALL, D), F32))
    outs = (struct((1, OWN, D), BF16), struct((1, OWN, D), F32)) + grads
    quarter = OWN // y_size
    v = pltpu.VMEM
    scratch = [v((LAYERS, D, WA), BF16), v((LAYERS, OWN + WU, D), BF16), v((SMALL, D), F32)]
    scratch += [v((LAYERS, 3) + group_shapes()[kind], BF16) for kind in KINDS]
    scratch += [v((LAYERS, 3) + shapes[kind], BF16) for kind in KINDS]
    scratch += [v((LAYERS,) + shapes[kind], BF16) for kind in KINDS]
    scratch += [
        v((SMALL, D), BF16),
        v((N - 1, SMALL, OWN), BF16),
        v((SMALL, OWN), BF16),
        v((REPLICAS - 1, SMALL, OWN), BF16),
    ]
    scratch += [
        v((LAYERS, N, y_size, quarter, WQ), BF16),
        v((LAYERS, N, y_size, quarter, WU), BF16),
        v((LAYERS, OWN, D), BF16),
        v((LAYERS, WU, D), BF16),
        v((SMALL, OWN), F32),
        v((SMALL, OWN), BF16),
        v((8, OWN), jnp.int32),
        v((N, SMALL, OWN), BF16),
        v((2 * N, 8, OWN), jnp.int32),
        v((SMALL, D), F32),
        v((8, D), F32),
        v((1, D), jnp.int32),
        v((2, 1, QB), F32),
        v((OWN, D), BF16),
        v((OWN, D), BF16),
        v((LAYERS, OWN, D), F32),
        v((LAYERS, GROUP, D), BF16),
        v((LAYERS, GROUP, WQ), BF16),
        v((LAYERS, 2, 1, GROUP), F32),
        v((LAYERS, GROUP, OWN), BF16),
        v((LAYERS, OWN, D), F32),
        v((LAYERS, GROUP, D), BF16),
        v((LAYERS, GROUP, WU), F32),
        v((LAYERS, GROUP, WU), BF16),
        v((GROUP, QB), F32),
        v((GROUP, QB), F32),
        v((OWN, GROUP), BF16),
        v((OWN, GROUP), F32),
        v((GROUP, D), BF16),
        v((GROUP, WU), BF16),
        v((GROUP, D), BF16),
        v((GROUP, OWN), BF16),
        v((GROUP, WQ), BF16),
        v((GROUP, OWN), F32),
        v((GROUP, OWN), F32),
        v((7 * OWN, D), BF16),
        v((7 * OWN, D), BF16),
        v((OWN, D), BF16),
        v((OWN, D), F32),
    ]
    copies = 4 * LAYERS * (GATHER_COPIES + SCATTER_COPIES) + 64
    return pl.pallas_call(
        functools.partial(blocks_kernel, y_size),
        out_shape=outs,
        in_specs=in_vmem(2) + [pl.BlockSpec(memory_space=pl.ANY)] * 4 + in_vmem(9),
        out_specs=in_vmem(2) + [pl.BlockSpec(memory_space=pl.ANY if whole else pltpu.VMEM)] * 4 + in_vmem(1),
        scratch_shapes=scratch + [pltpu.SemaphoreType.DMA((copies,)), pltpu.SemaphoreType.DMA((copies,))],
        compiler_params=pltpu.CompilerParams(collective_id=1, has_side_effects=True, vmem_limit_bytes=VMEM_LIMIT),
        cost_estimate=pl.CostEstimate(flops=24 << 30, bytes_accessed=32 << 20, transcendentals=16 << 20),
    )(*args)


ROWS = 32


def unpack_kernel(up, down, qkv, out, small, up_grad, down_grad, qkv_grad, out_grad,
                  g_gain1, g_shift1, g_gain2, g_shift2, g_out_bias, g_down_bias, g_qv_bias, g_up_bias):
    for l in range(LAYERS):
        here = slice(l, l + 1)
        singles = (g_gain1, g_shift1, g_gain2, g_shift2, g_out_bias, g_down_bias)
        for k, ref in enumerate(singles):
            ref[here, :] = small[16 * l + k : 16 * l + k + 1, :]
        for k in range(4):
            g_up_bias[here, k * OWN : (k + 1) * OWN] = small[16 * l + 6 + k : 16 * l + 7 + k, :]
        for k in range(2):
            g_qv_bias[here, k * OWN : (k + 1) * OWN] = small[16 * l + 10 + k : 16 * l + 11 + k, :]
    for w in range(N):
        up_grad[0, :, w * WU : (w + 1) * WU] = up[0, w, 0].astype(F32)
        for part in range(3):
            cols = slice(part * D + w * OWN, part * D + (w + 1) * OWN)
            qkv_grad[0, :, cols] = qkv[0, w, 0, :, part * OWN : (part + 1) * OWN].astype(F32)
    down_grad[0] = down[0].astype(F32)
    out_grad[0] = out[0].astype(F32)


def unpack(up, down, qkv, out, small):
    steps = OWN // ROWS
    per_half = HALF // ROWS

    def pieces(width):
        return pl.BlockSpec((1, N, 1, ROWS, width), lambda l, i: (l, 0, i // per_half, i % per_half, 0))

    def plain(rows, width):
        return pl.BlockSpec((1, rows, width), lambda l, i: (l, i, 0))

    def fixed(rows, width):
        return pl.BlockSpec((rows, width), lambda l, i: (0, 0))

    narrow = [OWN] * 6 + [2 * OWN, WU]
    return pl.pallas_call(
        unpack_kernel,
        grid=(LAYERS, steps),
        in_specs=[pieces(WU), plain(WU // steps, D), pieces(WQ), plain(ROWS, D), fixed(SMALL, OWN)],
        out_specs=[plain(ROWS, FF), plain(WU // steps, D), plain(ROWS, 3 * D), plain(ROWS, D)]
        + [fixed(LAYERS, width) for width in narrow],
        out_shape=[
            struct((LAYERS, OWN, FF), F32),
            struct((LAYERS, WU, D), F32),
            struct((LAYERS, OWN, 3 * D), F32),
            struct((LAYERS, OWN, D), F32),
        ]
        + [struct((LAYERS, width), F32) for width in narrow],
        compiler_params=pltpu.CompilerParams(vmem_limit_bytes=VMEM_LIMIT),
    )(up, down, qkv, out, small)


def per_device(y_size, reduce, tokens, segment_ids, cotangent, gain1, shift1, qkv_weight, qv_bias, out_weight, out_bias,
               gain2, shift2, up_weight, up_bias, down_weight, down_bias):
    output, grad, up, down, qkv, out, small = run_blocks(
        y_size, tokens, cotangent, qkv_weight, up_weight, out_weight, down_weight,
        gain1, shift1, out_bias, gain2, shift2, down_bias, qv_bias, up_bias, segment_ids,
    )
    if reduce is not None:
        up, down, qkv, out, small = reduce(up, down, small)
    up, down, qkv, out, g1, s1, g2, s2, ob, db, qv, ub = unpack(up, down, qkv, out, small)
    return output, grad, g1, s1, qkv, qv, out, ob, g2, s2, up, ub, down, db


def solution(mesh, reduce=None):
    rows = P(None, "shard")
    tiles = P(None, "shard", None)
    tokens = P("replica", "shard", None)
    y_size = 4 if mesh.shape["replica"] == REPLICAS else 1
    return jax.shard_map(
        functools.partial(per_device, y_size, reduce),
        mesh=mesh,
        in_specs=(
            tokens, P("replica", "shard"), tokens,
            rows, rows, tiles, rows, tiles, rows, rows, rows, tiles, rows, tiles, rows,
        ),
        out_specs=(tokens, tokens, rows, rows, tiles, rows, tiles, rows, rows, rows, tiles, rows, tiles, rows),
        check_vma=False,
    )
```

```python
import functools
import math

import jax
import jax.numpy as jnp
from jax import lax
from jax.experimental import pallas as pl
from jax.experimental.pallas import tpu as pltpu
from jax.sharding import PartitionSpec as P

D = 1024
H = 16
HD = 64
FF = 4096
LAYERS = 2
GROUP = 1024
OWN = 128
N = 8
WQ = 3 * D // N
WU = FF // N
WA = WQ + WU
QB = 256
KC = 128
MASKED = -1e30
EPS = 1e-5
MESH = pl.DeviceIdType.MESH
F32 = jnp.float32
BF16 = jnp.bfloat16
VMEM_LIMIT = 60 * 1024 * 1024

NN = (((1,), (0,)), ((), ()))
NT = (((1,), (1,)), ((), ()))
TN = (((0,), (0,)), ((), ()))


def dot(left, right, dims=NN):
    return lax.dot_general(left, right, dims, preferred_element_type=F32)


class Place:
    def __init__(self, y_size):
        self.shard = lax.axis_index("shard")
        self.replica = lax.axis_index("replica")
        self.side, self.z = self.shard // 4, self.shard % 4
        self.chip, self.core = self.replica // 2, self.replica % 2
        self.y_size = y_size
        self.y = self.chip % y_size
        self.block = self.core * 4 + self.z
        right, left, far = (self.z + 1) % 4, (self.z + 3) % 4, (self.z + 2) % 4
        self.right = {"shard": self.side * 4 + right}
        self.left = {"shard": self.side * 4 + left}
        self.twin = {"replica": self.chip * 2 + 1 - self.core}
        mine, other = self.core * 4, (1 - self.core) * 4
        self.right_block, self.left_block, self.far_block = mine + right, mine + left, mine + far
        self.twin_block = other + self.z
        self.twin_right, self.twin_left, self.twin_far = other + right, other + left, other + far
        opposite = (1 - self.side) * 4 + self.z
        self.partner = {"shard": opposite, "replica": self.chip * 2 + 1 - self.core}
        self.needs_x = {"shard": opposite, "replica": self.chip * 2 + self.side}
        self.moves = self.core != self.side

    def at_shard(self, j):
        return {"shard": (self.shard + j) % N}

    def at_block(self, flip, j):
        core = self.core if flip == 0 else 1 - self.core
        return {"shard": (self.shard + j) % N, "replica": self.chip * 2 + core}

    def at_y(self, j):
        chip = self.chip - self.y + (self.y + j) % self.y_size
        return {"replica": chip * 2 + self.core}

    def greet(self, replicas, meanwhile):
        barrier = pltpu.get_barrier_semaphore()
        for i in range(N):
            for j in range(replicas):
                if i + j > 0:
                    peer = {"shard": (self.shard + i) % N, "replica": (self.replica + j) % replicas}
                    pl.semaphore_signal(barrier, inc=1, device_id=peer, device_id_type=MESH)
        meanwhile()
        pl.semaphore_wait(barrier, N * replicas - 1)


def block(index, rows=OWN, start=0):
    return pl.ds(pl.multiple_of(index * OWN + start, 16), rows)


def lanes_of(index):
    return pl.ds(pl.multiple_of(index * OWN, OWN), OWN)


class Links:
    def __init__(self, send_sems, recv_sems):
        self.send_sems, self.recv_sems, self.used = send_sems, recv_sems, 0

    def pair(self, count=1):
        index = self.used
        self.used += count
        return index

    def make(self, src, dst, peer, send, recv):
        return pltpu.make_async_remote_copy(
            src_ref=src,
            dst_ref=dst,
            send_sem=self.send_sems.at[send],
            recv_sem=self.recv_sems.at[recv],
            device_id=peer,
            device_id_type=MESH,
        )

    def copy(self, src, dst, peer):
        index = self.pair()
        copy = self.make(src, dst, peer, index, index)
        copy.start()
        return copy

    def local(self, src, dst, recv):
        pltpu.make_async_copy(src, dst, self.recv_sems.at[recv]).start()

    def landed(self, ref, recv):
        pltpu.make_async_copy(ref, ref, self.recv_sems.at[recv]).wait()

    def sent(self, ref, send):
        pltpu.make_async_copy(ref, ref, self.send_sems.at[send]).wait()


def gather(links, place, full, use):
    p = place
    half = OWN // 2

    def send(index, peer, rows=OWN, start=0):
        ref = full.at[block(index, rows, start), :]
        return links.copy(ref, ref, peer)

    low_r = send(p.block, p.right, half, 0)
    high_l = send(p.block, p.left, half, half)
    own_t = send(p.block, p.twin)
    high_r = send(p.block, p.right, half, half)
    low_l = send(p.block, p.left, half, 0)
    use(p.block)
    own_t.wait_recv()
    use(p.twin_block)
    low_r.wait_recv()
    far_low = send(p.left_block, p.right, half, 0)
    high_l.wait_recv()
    far_high = send(p.right_block, p.left, half, half)
    high_r.wait_recv()
    left_t = send(p.left_block, p.twin)
    low_l.wait_recv()
    right_t = send(p.right_block, p.twin)
    use(p.left_block)
    use(p.right_block)
    left_t.wait_recv()
    use(p.twin_left)
    right_t.wait_recv()
    use(p.twin_right)
    far_low.wait_recv()
    low_t = send(p.far_block, p.twin, half, 0)
    far_high.wait_recv()
    high_t = send(p.far_block, p.twin, half, half)
    use(p.far_block)
    low_t.wait_recv()
    high_t.wait_recv()
    use(p.twin_far)
    for copy in (low_r, high_l, own_t, high_r, low_l, far_low, far_high, left_t, right_t, low_t, high_t):
        copy.wait_send()


GATHER_COPIES = 11


def scatter(links, place, make, out, slots, beside=()):
    p = place
    half = OWN // 2
    beside = list(beside) + [lambda: None] * 2

    def rows_of(role, rows=OWN, start=0):
        return pl.ds(role * OWN + start, rows)

    def send(role, slot, peer, rows=OWN, start=0):
        return links.copy(out.at[rows_of(role, rows, start), :], slots.at[rows_of(slot, rows, start), :], peer)

    def fill(role, index):
        out[rows_of(role), :] = make(index).astype(BF16)

    def add(role, slot, rows=OWN, start=0):
        mine, theirs = rows_of(role, rows, start), rows_of(slot, rows, start)
        out[mine, :] = (out[mine, :].astype(F32) + slots[theirs, :].astype(F32)).astype(BF16)

    twins = []
    for role, index in enumerate((p.twin_far, p.twin_right, p.twin_left, p.twin_block)):
        fill(role, index)
        twins.append(send(role, role, p.twin))
    fill(4, p.far_block)
    twins[0].wait_recv()
    add(4, 0)
    far_low = send(4, 4, p.right, half, 0)
    far_high = send(4, 4, p.left, half, half)
    fill(5, p.right_block)
    twins[1].wait_recv()
    add(5, 1)
    high_r = send(5, 5, p.right, half, half)
    fill(6, p.left_block)
    twins[2].wait_recv()
    add(6, 2)
    low_l = send(6, 6, p.left, half, 0)
    own = make(p.block)
    twins[3].wait_recv()
    own = own + slots[rows_of(3), :].astype(F32)
    beside[0]()
    far_low.wait_recv()
    add(5, 4, half, 0)
    low_r = send(5, 5, p.right, half, 0)
    far_high.wait_recv()
    add(6, 4, half, half)
    high_l = send(6, 6, p.left, half, half)
    beside[1]()
    for copy in (high_r, low_l, low_r, high_l):
        copy.wait_recv()
    own = own + slots[rows_of(5), :].astype(F32) + slots[rows_of(6), :].astype(F32)
    for copy in twins + [far_low, far_high, high_r, low_l, low_r, high_l]:
        copy.wait_send()
    return own


SCATTER_COPIES = 10


def standardize(rows):
    mean = jnp.mean(rows, axis=-1, keepdims=True)
    centered = rows - mean
    variance = jnp.mean(centered * centered, axis=-1, keepdims=True)
    scale = lax.rsqrt(variance + EPS)
    return centered * scale, scale


def normalize_back(rows, gain, grad):
    unit, scale = standardize(rows)
    d_unit = grad * gain
    mean = jnp.mean(d_unit, axis=-1, keepdims=True)
    along = jnp.mean(d_unit * unit, axis=-1, keepdims=True)
    d_rows = scale * (d_unit - mean - unit * along)
    d_gain = jnp.sum(grad * unit, axis=0, keepdims=True)
    d_shift = jnp.sum(grad, axis=0, keepdims=True)
    return d_rows, d_gain, d_shift


def gelu_pair(u):
    c = math.sqrt(2.0 / math.pi)
    square = u * u
    t = jnp.tanh(c * (u + 0.044715 * u * square))
    value = 0.5 * u * (1.0 + t)
    slope = 0.5 * (1.0 + t) + 0.5 * u * (1.0 - t * t) * (c * (1.0 + 3.0 * 0.044715 * square))
    return value, slope


def head_lanes(rows, head):
    lane = lax.broadcasted_iota(jnp.int32, (1, 2 * HD), 1)
    keep = (lane // HD) == head
    return jnp.where(keep, rows, jnp.zeros_like(rows))


def masked_scores(keys, query, slope, start, chunk, block_start, edge):
    scores = dot(keys, query, NT)
    row = lax.broadcasted_iota(jnp.int32, scores.shape, 0) + chunk
    scores = scores + slope * (row - block_start).astype(F32)
    keep = row >= start
    if edge:
        col = lax.broadcasted_iota(jnp.int32, scores.shape, 1) + block_start
        keep = keep & (row <= col)
    return jnp.where(keep, scores, MASKED)


class Weights:
    def __init__(self, links, place, raw, full):
        self.links, self.p = links, place
        self.raw, self.full = raw, full
        self.rows = OWN // place.y_size
        self.first = links.pair(4)
        self.second = links.pair(4)
        self.x = links.pair(4)

    def pieces(self, kind, l, peer_shard):
        p = self.p
        rows = pl.ds(pl.multiple_of(p.y * self.rows, 16), self.rows)
        take = p.core * 4 + peer_shard % 4
        dst = self.full[kind].at[l, p.shard, p.y]
        if kind == 0:
            for part in range(3):
                cols = pl.ds(pl.multiple_of(part * D + take * OWN, OWN), OWN)
                yield self.raw[0].at[l, rows, cols], dst.at[:, part * OWN : (part + 1) * OWN]
        else:
            yield self.raw[1].at[l, rows, pl.ds(pl.multiple_of(take * WU, OWN), WU)], dst

    def start(self, kind, l):
        sem = self.first + l * 2 + kind
        for j in range(1, N):
            peer = (self.p.shard + j) % N
            for src, dst in self.pieces(kind, l, peer):
                self.links.make(src, dst, {"shard": peer}, sem, sem).start()
        for src, dst in self.pieces(kind, l, self.p.shard):
            self.links.local(src, dst, sem)

    def around(self, kind, l):
        full = self.full[kind].at[l]
        self.links.landed(full.at[:, 0], self.first + l * 2 + kind)
        sem = self.second + l * 2 + kind
        for j in range(1, self.p.y_size):
            self.links.make(full.at[:, self.p.y], full.at[:, self.p.y], self.p.at_y(j), sem, sem).start()

    def ready(self, kind, l):
        if self.p.y_size > 1:
            self.links.landed(self.full[kind].at[l, :, 0 : self.p.y_size - 1], self.second + l * 2 + kind)

    def start_x(self):
        p = self.p
        for k in (2, 3):
            sem = self.x + (k - 2) * 2
            self.links.make(self.raw[k].at[p.core], self.full[k].at[p.core], p.needs_x, sem, sem + p.core).start()

        @pl.when(jnp.logical_not(p.moves))
        def _():
            for k in (2, 3):
                for l in range(LAYERS):
                    self.links.local(self.raw[k].at[l], self.full[k].at[l], self.x + (k - 2) * 2 + l)

    def ready_x(self, kind, l):
        self.links.landed(self.full[kind].at[l], self.x + (kind - 2) * 2 + l)

    def finish(self):
        for l in range(LAYERS):
            for kind in (0, 1):
                full = self.full[kind].at[l]
                self.links.sent(full.at[0 : N - 1, 0], self.first + l * 2 + kind)
                if self.p.y_size > 1:
                    self.links.sent(full.at[:, 0 : self.p.y_size - 1], self.second + l * 2 + kind)
        for k in (2, 3):
            self.links.sent(self.full[k].at[0], self.x + (k - 2) * 2)


class Swap:
    def __init__(self, links, place, src, dst):
        self.links, self.p, self.dst = links, place, dst
        self.sem = links.pair()
        self.copy = links.make(src, dst, place.partner, self.sem, self.sem)

        @pl.when(place.moves)
        def _():
            self.copy.start()

        @pl.when(jnp.logical_not(place.moves))
        def _():
            links.local(src, dst, self.sem)

    def ready(self):
        self.links.landed(self.dst, self.sem)

    def finish(self):
        @pl.when(self.p.moves)
        def _():
            self.copy.wait_send()


REPLICAS = 16
CHIPS = 8
HALF = OWN // 2
KINDS = ("up", "down", "qkv", "out")


class Sums:
    def __init__(self, links, place, l, wide, tall, wholes, slots, totals, outs):
        self.links, self.p, self.l = links, place, l
        self.wide, self.tall = wide, tall
        self.wholes, self.slots, self.totals, self.outs = wholes, slots, totals, outs
        self.along_x = place.side * 2 + place.chip // 4
        self.along_y = place.chip % 4
        self.around = links.pair(len(KINDS))
        self.sems = links.pair(len(KINDS))
        self.give = links.pair(len(KINDS))
        self.twin = links.pair(len(KINDS))
        self.last = {}

    def first(self, kind):
        return self.along_x if by_rows(kind) else self.along_y

    def second(self, kind):
        return self.along_y if by_rows(kind) else self.along_x

    def number(self, kind):
        return self.first(kind) * 4 + self.second(kind)

    def at(self, x, y):
        return {"shard": (x // 2) * 4 + self.p.z, "replica": ((x % 2) * 4 + y) * 2 + self.p.core}

    def group(self, kind, first):
        if by_rows(kind):
            cols = slice(WQ, WA) if kind == "up" else slice(0, WQ)
            return self.wide.at[self.l, block_of(first, 4 * HALF), cols]
        rows = WU // 4 if kind == "down" else OWN // 4
        start = OWN if kind == "down" else 0
        return self.tall.at[self.l, pl.ds(pl.multiple_of(start + first * rows, 16), rows), :]

    def part(self, kind, q):
        if by_rows(kind):
            cols = slice(WQ, WA) if kind == "up" else slice(0, WQ)
            return self.wide.at[self.l, block_of(q, HALF), cols]
        rows = WU // 8 if kind == "down" else OWN // 8
        start = OWN if kind == "down" else 0
        return self.tall.at[self.l, pl.ds(pl.multiple_of(start + (q // 2) * rows, 16), rows), half_of(q % 2)]

    def target(self, kind):
        out, q = self.outs[kind], self.number(kind)
        if by_rows(kind):
            return out.at[self.l, self.p.block, q % 2]
        rows = WU // 8 if kind == "down" else OWN // 8
        return out.at[self.l, block_of(q // 2, rows), half_of(q % 2)]

    def region(self, kind, core):
        out = self.outs[kind]
        return out.at[self.l, pl.ds(core * 4, 4)] if by_rows(kind) else out.at[self.l, :, half_of(core)]

    def start(self, *kinds):
        for kind in kinds:
            sem = self.around + KINDS.index(kind)
            for j in range(1, 4):
                other = (self.first(kind) + j) % 4
                peer = self.at(other, self.along_y) if by_rows(kind) else self.at(self.along_x, other)
                self.links.make(self.group(kind, other), self.wholes[kind].at[j - 1], peer, sem, sem).start()

    def middle(self, *kinds):
        for kind in kinds:
            wholes = self.wholes[kind]
            self.links.landed(wholes, self.around + KINDS.index(kind))
            group = self.group(kind, self.first(kind))
            total = group[...].astype(F32)
            for j in range(3):
                total = total + wholes[j].astype(F32)
            group[...] = total.astype(BF16)
            sem = self.sems + KINDS.index(kind)
            for j in range(1, 4):
                other = (self.second(kind) + j) % 4
                peer = self.at(self.along_x, other) if by_rows(kind) else self.at(other, self.along_y)
                part = self.part(kind, self.first(kind) * 4 + other)
                self.links.make(part, self.slots[kind].at[j - 1], peer, sem, sem).start()

    def total(self, *kinds):
        for kind in kinds:
            slots, q = self.slots[kind], self.number(kind)
            self.links.landed(slots, self.sems + KINDS.index(kind))
            part = self.part(kind, q)[...].astype(F32)
            for j in range(3):
                part = part + slots[j].astype(F32)
            self.totals[kind][...] = part.astype(BF16)
            sem = self.give + KINDS.index(kind)
            shard = q // 2 if by_rows(kind) else self.p.block
            core = self.p.core if by_rows(kind) else q % 2
            target = self.target(kind)
            for j in range(1, CHIPS):
                peer = {"shard": shard, "replica": ((self.p.chip + j) % CHIPS) * 2 + core}
                self.links.make(self.totals[kind], target, peer, sem, sem).start()
            mine = (shard == self.p.shard) & (core == self.p.core)
            last = self.links.make(self.totals[kind], target, {"shard": shard, "replica": self.p.chip * 2 + core}, sem, sem)
            pl.when(mine)(functools.partial(self.links.local, self.totals[kind], target, sem))
            pl.when(jnp.logical_not(mine))(last.start)
            self.last[kind] = (mine, last)

    def share(self, *kinds):
        for kind in kinds:
            region = self.region(kind, self.p.core)
            self.links.landed(region, self.give + KINDS.index(kind))
            self.links.make(region, region, self.p.twin, self.twin + KINDS.index(kind), self.twin + KINDS.index(kind)).start()

    def finish(self):
        for kind in KINDS:
            index = KINDS.index(kind)
            region = self.region(kind, self.p.core)
            self.links.landed(region, self.twin + index)
            self.links.sent(region, self.twin + index)
            self.links.sent(self.wholes[kind], self.around + index)
            self.links.sent(self.slots[kind], self.sems + index)
            out = self.outs[kind]
            rows = (CHIPS - 1) * self.totals[kind].shape[0]
            given = out.at[self.l, 0 : CHIPS - 1, 0] if by_rows(kind) else out.at[self.l, 0:rows, 0 : D // 2]
            self.links.sent(given, self.give + index)
            mine, last = self.last[kind]
            pl.when(jnp.logical_not(mine))(last.wait_send)


def by_rows(kind):
    return kind in ("up", "qkv")


def block_of(index, rows):
    return pl.ds(pl.multiple_of(index * rows, 16), rows)


def half_of(index):
    return pl.ds(pl.multiple_of(index * (D // 2), OWN), D // 2)


def group_shapes():
    return {"up": (4 * HALF, WU), "down": (WU // 4, D), "qkv": (4 * HALF, WQ), "out": (OWN // 4, D)}


def part_shapes():
    return {"up": (HALF, WU), "down": (WU // 8, D // 2), "qkv": (HALF, WQ), "out": (OWN // 8, D // 2)}


class SmallSums:
    def __init__(self, links, place, mine, low, slots, total, everyone, out):
        self.links, self.p = links, place
        self.mine, self.low, self.slots, self.sum, self.everyone, self.out = mine, low, slots, total, everyone, out
        self.first, self.second = links.pair(), links.pair()

    def start(self):
        self.low[...] = self.mine[...].astype(BF16)
        for j in range(1, N):
            peer = self.p.at_shard(j)
            src = self.low.at[:, lanes_of(peer["shard"])]
            self.links.make(src, self.slots.at[j - 1], peer, self.first, self.first).start()

    def total(self):
        self.links.landed(self.slots, self.first)
        total = self.mine[:, lanes_of(self.p.shard)]
        for j in range(N - 1):
            total = total + self.slots[j].astype(F32)
        self.sum[...] = total.astype(BF16)
        for j in range(1, REPLICAS):
            peer = {"replica": (self.p.replica + j) % REPLICAS}
            self.links.make(self.sum, self.everyone.at[j - 1], peer, self.second, self.second).start()

    def finish(self):
        self.links.landed(self.everyone, self.second)
        total = self.sum[...].astype(F32)
        for j in range(REPLICAS - 1):
            total = total + self.everyone[j].astype(F32)
        self.out[...] = total
        self.links.sent(self.slots, self.first)
        self.links.sent(self.everyone, self.second)


def blocks_kernel(
    y_size,
    tokens, cotangent, raw_qkv, raw_up, raw_out, raw_down, gain1, shift1, out_bias, gain2, shift2, down_bias,
    qv_bias, up_bias, own_ids,
    output, tokens_grad, up_out, down_out, qkv_out, out_out, small_out,
    wide, tall, mine, up_groups, down_groups, qkv_groups, out_groups, up_slots, down_slots, qkv_slots, out_slots, up_sum, down_sum, qkv_sum, out_sum,
    small_low, small_slots, small_sum, small_every,
    w_qkv, w_up, w_out, w_down, small_wide, small, segs, small_all, segs_all, vectors, ids, starts, slopes,
    token_in, cot_in, state, hidden1, qkv, lse, mixed, middle, hidden2, act_slope, active,
    score_scr, dprob_scr, turned, mixed_turned, d_full, d_upped, branch, d_mixed, d_qkv, dk_acc, dv_acc,
    out_scr, slots, low_out, grad, send_sems, recv_sems,
):
    place = Place(y_size)
    links = Links(send_sems, recv_sems)
    own = block(place.block)
    lanes = lanes_of(place.block)
    factor = 1.0 / math.sqrt(HD)
    whole = y_size > 1

    def pack():
        small_wide[...] = jnp.zeros_like(small_wide)
        for l in range(LAYERS):
            for k, ref in enumerate((gain1, shift1, out_bias, gain2, shift2, down_bias)):
                small_wide[6 * l + k : 6 * l + k + 1, :] = ref[l : l + 1, :].astype(F32)
            for k in range(2):
                small_wide[12 + 2 * l + k : 13 + 2 * l + k, :] = qv_bias[l : l + 1, k * OWN : (k + 1) * OWN].astype(F32)
            for k in range(4):
                small_wide[16 + 4 * l + k : 17 + 4 * l + k, :] = up_bias[l : l + 1, k * OWN : (k + 1) * OWN].astype(F32)
        small[...] = small_wide[...].astype(BF16)
        segs[...] = jnp.broadcast_to(own_ids[...], segs.shape)

    place.greet(REPLICAS if whole else 2, pack)
    weights = Weights(links, place, (raw_qkv, raw_up, raw_out, raw_down), (w_qkv, w_up, w_out, w_down))
    small_sem, segs_sem = links.pair(), links.pair()
    swap_tokens = Swap(links, place, tokens.at[0], token_in)
    for j in range(1, N):
        links.make(small, small_all.at[place.shard], place.at_shard(j), small_sem, small_sem).start()
    links.local(small, small_all.at[place.shard], small_sem)
    weights.start(0, 0)
    here = place.core * N + place.shard
    for flip in range(2):
        for j in range(N):
            if flip + j > 0:
                links.make(segs, segs_all.at[here], place.at_block(flip, j), segs_sem, segs_sem).start()
    links.local(segs, segs_all.at[here], segs_sem)
    links.landed(small_all, small_sem)
    for s in range(N):
        vectors[:, s * OWN : (s + 1) * OWN] = small_all[s].astype(F32)
    swap_tokens.ready()
    state[0] = token_in[...].astype(F32)
    for head in range(2):
        power = (place.block * 2 + head + 1).astype(F32) * (-8.0 / H * math.log(2.0))
        slopes[head] = jnp.exp(jnp.full((1, QB), power, F32))
    outs = dict(zip(KINDS, (up_out, down_out, qkv_out, out_out)))
    parts = dict(zip(KINDS, (up_slots, down_slots, qkv_slots, out_slots)))
    groups = dict(zip(KINDS, (up_groups, down_groups, qkv_groups, out_groups)))
    totals = dict(zip(KINDS, (up_sum, down_sum, qkv_sum, out_sum)))
    sums = [None] * LAYERS
    for l in range(LAYERS):
        if whole:
            own_parts = {k: ref.at[l] for k, ref in parts.items()}
            own_groups = {k: ref.at[l] for k, ref in groups.items()}
            own_totals = {k: ref.at[l] for k, ref in totals.items()}
            sums[l] = Sums(links, place, l, wide, tall, own_groups, own_parts, own_totals, outs)
    smalls = SmallSums(links, place, mine, small_low, small_slots, small_sum, small_every, small_out)
    mine[...] = jnp.zeros_like(mine)

    def vector(l, k):
        return vectors[l * 6 + k : l * 6 + k + 1, :]

    def q_or_v_bias(l, base):
        cols = lanes_of(base + place.block // 2)
        even, odd = (vectors[12 + 2 * l + k : 13 + 2 * l + k, cols] for k in range(2))
        return jnp.where(place.block % 2 == 0, even, odd)

    def weight(ref, l, cols):
        return ref[l].reshape(D, cols)

    for l in range(LAYERS):
        rows_in = state[l]
        hidden1[l, own, :] = (standardize(rows_in)[0] * vector(l, 0) + vector(l, 1)).astype(BF16)
        if l == 0:
            landing = []

            def fetch(index, landing=landing):
                if not landing:
                    weights.around(0, 0)
                    weights.start(1, 0)
                    weights.start(0, 1)
                    weights.start(1, 1)
                    weights.start_x()
                landing.append(index)
        bias = jnp.concatenate([q_or_v_bias(l, 0), jnp.zeros((1, OWN), F32), q_or_v_bias(l, 4)], axis=1)

        def project(index, l=l, bias=bias):
            rows = block(index)
            qkv[l, rows, :] = (dot(hidden1[l, rows, :], weight(w_qkv, l, WQ)) + bias).astype(BF16)

        if l == 0:
            gather(links, place, hidden1.at[l], fetch)
            swap_cot = Swap(links, place, cotangent.at[0], cot_in)
            weights.ready(0, 0)
            for index in landing:
                project(index)
            links.landed(segs_all, segs_sem)
            for s in range(N):
                ids[:, s * OWN : (s + 1) * OWN] = segs_all[place.side * N + s].astype(F32)
            row = ids[0:1, :]
            start = jnp.zeros((1, GROUP), F32)
            for value in range(3):
                count = jnp.sum(jnp.where(row == value, 1.0, 0.0), axis=1, keepdims=True)
                start = start + jnp.where(row > value, count, 0.0)
            starts[...] = start.astype(jnp.int32)
        else:
            gather(links, place, hidden1.at[l], project)

        turned[...] = qkv[l, :, 2 * OWN : 3 * OWN].T

        def attend(head, carry, l=l):
            slope = slopes[head]
            own_v = pl.ds(pl.multiple_of(head * HD, HD), HD)
            for qb in range(GROUP // QB):
                cols = slice(qb * QB, (qb + 1) * QB)
                query = head_lanes(qkv[l, cols, 0:OWN], head) * jnp.asarray(factor, BF16)
                start = starts[:, cols]
                top = jnp.full((1, QB), MASKED, F32)
                chunks = (qb + 1) * QB // KC
                for c in range(chunks):
                    keys = slice(c * KC, (c + 1) * KC)
                    edge = (c + 1) * KC > qb * QB
                    s = masked_scores(qkv[l, keys, OWN : 2 * OWN], query, slope, start, c * KC, qb * QB, edge)
                    score_scr[keys, :] = s
                    top = jnp.maximum(top, jnp.max(s, axis=0, keepdims=True))
                total = jnp.zeros((1, QB), F32)
                acc = jnp.zeros((HD, QB), F32)
                for c in range(chunks):
                    keys = slice(c * KC, (c + 1) * KC)
                    e = jnp.exp(score_scr[keys, :] - top)
                    total = total + jnp.sum(e, axis=0, keepdims=True)
                    acc = acc + dot(turned[own_v, keys], e.astype(BF16))
                mixed_turned[own_v, cols] = acc / total
                lse[l, head, :, cols] = top + jnp.log(total)
            return carry

        if l == 0:
            weights.around(1, 0)
        lax.fori_loop(0, 2, attend, 0)
        mixed[l] = mixed_turned[...].T.astype(BF16)
        weights.ready_x(2, l)
        if l == 0:
            weights.around(0, 1)
            weights.around(1, 1)

        def out_part(index, l=l):
            return dot(mixed[l, block(index), :], w_out[l])

        middle[l] = state[l] + scatter(links, place, out_part, out_scr, slots) + vector(l, 2)
        hidden2[l, own, :] = (standardize(middle[l])[0] * vector(l, 3) + vector(l, 4)).astype(BF16)
        weights.ready(1, l)
        up_bias = jnp.concatenate([vectors[16 + 4 * l + k : 17 + 4 * l + k, lanes] for k in range(4)], axis=1)

        def up(index, l=l, up_bias=up_bias):
            rows = block(index)
            value, slope = gelu_pair(dot(hidden2[l, rows, :], weight(w_up, l, WU)) + up_bias)
            active[l, rows, :] = value.astype(BF16)
            act_slope[l, rows, :] = slope

        gather(links, place, hidden2.at[l], up)
        weights.ready_x(3, l)

        def down_part(index, l=l):
            return dot(active[l, block(index), :], w_down[l])

        result = middle[l] + scatter(links, place, down_part, out_scr, slots) + vector(l, 5)
        if l + 1 < LAYERS:
            state[l + 1] = result
            weights.ready(0, l + 1)
        else:
            low_out[...] = result.astype(BF16)
    swap_output = Swap(links, place, low_out, output.at[0])
    swap_cot.ready()
    grad[...] = cot_in[...].astype(F32)

    for l in reversed(range(LAYERS)):
        d_full[own, :] = grad[...].astype(BF16)

        def down_back(index, l=l):
            rows = block(index)
            d_upped[rows, :] = (dot(d_full[rows, :], w_down[l], NT) * act_slope[l, rows, :]).astype(BF16)

        gather(links, place, d_full, down_back)

        def up_back(index, l=l):
            return dot(d_upped[block(index), :], weight(w_up, l, WU), NT)

        def down_grads(l=l):
            def step(i, carry):
                cols = lanes_of(i)
                tall[l, lanes_of(1 + i), :] = dot(active[l, :, cols], d_full[...], TN).astype(BF16)
                return carry

            lax.fori_loop(0, WU // OWN, step, 0)
            if whole:
                sums[l].start("down")
            mine[16 * l + 5 : 16 * l + 6, lanes] = jnp.sum(d_full[:, lanes].astype(F32), axis=0, keepdims=True)

        def up_grads(l=l):
            def step(i, carry):
                cols = lanes_of(i)
                wide[l, cols, WQ:WA] = dot(hidden2[l, :, cols], d_upped[...], TN).astype(BF16)
                return carry

            lax.fori_loop(0, D // OWN, step, 0)
            if whole:
                sums[l].start("up")
                if l + 1 < LAYERS:
                    sums[l + 1].total("down", "up")
                    sums[l + 1].middle("out", "qkv")
            total = jnp.sum(d_upped[...].astype(F32), axis=0, keepdims=True)
            for k in range(WU // OWN):
                mine[16 * l + 6 + k : 16 * l + 7 + k, lanes] = total[:, k * OWN : (k + 1) * OWN]

        d_hidden2 = scatter(links, place, up_back, out_scr, slots, (down_grads, up_grads))
        d_rows, d_gain, d_shift = normalize_back(middle[l], vector(l, 3), d_hidden2)
        mine[16 * l + 2 : 16 * l + 3, :] = d_gain
        mine[16 * l + 3 : 16 * l + 4, :] = d_shift
        grad[...] += d_rows
        branch[own, :] = grad[...].astype(BF16)

        def out_back(index, l=l):
            rows = block(index)
            d_mixed[rows, :] = dot(branch[rows, :], w_out[l], NT).astype(BF16)

        gather(links, place, branch, out_back)
        if whole and l + 1 < LAYERS:
            sums[l + 1].total("out", "qkv")
            sums[l + 1].share("down", "up")

        turned[...] = qkv[l, :, OWN : 2 * OWN].T
        dk_acc[...] = jnp.zeros_like(dk_acc)
        dv_acc[...] = jnp.zeros_like(dv_acc)

        def attend_back(head, carry, l=l):
            slope = slopes[head]
            own_k = pl.ds(pl.multiple_of(head * HD, HD), HD)
            for qb in range(GROUP // QB):
                cols = slice(qb * QB, (qb + 1) * QB)
                query = head_lanes(qkv[l, cols, 0:OWN], head) * jnp.asarray(factor, BF16)
                d_mix = head_lanes(d_mixed[cols, :], head)
                start = starts[:, cols]
                log_total = lse[l, head, :, cols]
                delta = jnp.zeros((1, QB), F32)
                chunks = (qb + 1) * QB // KC
                for c in range(chunks):
                    keys = slice(c * KC, (c + 1) * KC)
                    edge = (c + 1) * KC > qb * QB
                    s = masked_scores(qkv[l, keys, OWN : 2 * OWN], query, slope, start, c * KC, qb * QB, edge)
                    prob = jnp.exp(s - log_total)
                    d_prob = dot(qkv[l, keys, 2 * OWN : 3 * OWN], d_mix, NT)
                    delta = delta + jnp.sum(prob * d_prob, axis=0, keepdims=True)
                    score_scr[keys, :] = prob
                    dprob_scr[keys, :] = d_prob
                    dv_acc[keys, :] += dot(prob.astype(BF16), d_mix)
                acc = jnp.zeros((HD, QB), F32)
                for c in range(chunks):
                    keys = slice(c * KC, (c + 1) * KC)
                    d_score = (score_scr[keys, :] * (dprob_scr[keys, :] - delta)).astype(BF16)
                    dk_acc[keys, :] += dot(d_score, query)
                    acc = acc + dot(turned[own_k, keys], d_score)
                mixed_turned[own_k, cols] = acc * factor
            return carry

        lax.fori_loop(0, 2, attend_back, 0)
        d_qkv[:, 0:OWN] = mixed_turned[...].T.astype(BF16)
        d_qkv[:, OWN : 2 * OWN] = dk_acc[...].astype(BF16)
        d_qkv[:, 2 * OWN : 3 * OWN] = dv_acc[...].astype(BF16)

        def qkv_back(index, l=l):
            rows = block(index)
            w = weight(w_qkv, l, WQ)
            both = dot(d_qkv[rows, 0 : 2 * OWN], w[:, 0 : 2 * OWN], NT)
            return both + dot(d_qkv[rows, 2 * OWN : 3 * OWN], w[:, 2 * OWN : 3 * OWN], NT)

        def qkv_grads(l=l):
            def step(i, carry):
                cols = lanes_of(i)
                wide[l, cols, 0:WQ] = dot(hidden1[l, :, cols], d_qkv[...], TN).astype(BF16)
                return carry

            lax.fori_loop(0, D // OWN, step, 0)
            if whole:
                sums[l].start("qkv")
                sums[l].middle("down", "up")

        def out_grads(l=l):
            tall[l, 0:OWN, :] = dot(mixed[l], branch[...], TN).astype(BF16)
            if whole:
                sums[l].start("out")
                if l + 1 < LAYERS:
                    sums[l + 1].share("out", "qkv")
            mine[16 * l + 4 : 16 * l + 5, lanes] = jnp.sum(branch[:, lanes].astype(F32), axis=0, keepdims=True)
            total = jnp.sum(d_qkv[...].astype(F32), axis=0, keepdims=True)
            for first, base in ((0, 0), (2 * OWN, 4)):
                bias = total[:, first : first + OWN]
                cols = lanes_of(base + place.block // 2)
                for k in range(2):
                    mine[16 * l + 10 + k : 16 * l + 11 + k, cols] = jnp.where(place.block % 2 == k, bias, 0.0)

        d_hidden1 = scatter(links, place, qkv_back, out_scr, slots, (qkv_grads, out_grads))
        d_rows, d_gain, d_shift = normalize_back(state[l], vector(l, 0), d_hidden1)
        mine[16 * l + 0 : 16 * l + 1, :] = d_gain
        mine[16 * l + 1 : 16 * l + 2, :] = d_shift
        grad[...] += d_rows

    swap_grad = Swap(links, place, grad, tokens_grad.at[0])
    if whole:
        smalls.start()
        sums[0].total("down", "up")
        sums[0].middle("out", "qkv")
        smalls.total()
        sums[0].total("out", "qkv")
        sums[0].share("down", "up")
        smalls.finish()
        sums[0].share("out", "qkv")
    else:
        up_out[...] = wide[...]
        down_out[...] = tall[...]
        small_out[...] = mine[...]
    swap_output.ready()
    swap_grad.ready()
    weights.finish()
    links.sent(small_all.at[0 : N - 1], small_sem)
    links.sent(segs_all.at[0 : 2 * N - 1], segs_sem)
    for swap in (swap_tokens, swap_cot, swap_output, swap_grad):
        swap.finish()
    if whole:
        for layer in sums:
            layer.finish()


def in_vmem(count):
    return [pl.BlockSpec(memory_space=pltpu.VMEM)] * count


def struct(shape, dtype):
    return jax.ShapeDtypeStruct(shape, dtype)


SMALL = 32


def run_blocks(y_size, *args):
    whole = y_size > 1
    shapes = part_shapes()
    if whole:
        grads = (
            struct((LAYERS, N, 2, HALF, WU), BF16),
            struct((LAYERS, WU, D), BF16),
            struct((LAYERS, N, 2, HALF, WQ), BF16),
            struct((LAYERS, OWN, D), BF16),
            struct((SMALL, OWN), F32),
        )
    else:
        empty = struct((8, OWN), F32)
        grads = (struct((LAYERS, D, WA), BF16), struct((LAYERS, OWN + WU, D), BF16), empty, empty, struct((SMALL, D), F32))
    outs = (struct((1, OWN, D), BF16), struct((1, OWN, D), F32)) + grads
    quarter = OWN // y_size
    v = pltpu.VMEM
    scratch = [v((LAYERS, D, WA), BF16), v((LAYERS, OWN + WU, D), BF16), v((SMALL, D), F32)]
    scratch += [v((LAYERS, 3) + group_shapes()[kind], BF16) for kind in KINDS]
    scratch += [v((LAYERS, 3) + shapes[kind], BF16) for kind in KINDS]
    scratch += [v((LAYERS,) + shapes[kind], BF16) for kind in KINDS]
    scratch += [
        v((SMALL, D), BF16),
        v((N - 1, SMALL, OWN), BF16),
        v((SMALL, OWN), BF16),
        v((REPLICAS - 1, SMALL, OWN), BF16),
    ]
    scratch += [
        v((LAYERS, N, y_size, quarter, WQ), BF16),
        v((LAYERS, N, y_size, quarter, WU), BF16),
        v((LAYERS, OWN, D), BF16),
        v((LAYERS, WU, D), BF16),
        v((SMALL, OWN), F32),
        v((SMALL, OWN), BF16),
        v((8, OWN), jnp.int32),
        v((N, SMALL, OWN), BF16),
        v((2 * N, 8, OWN), jnp.int32),
        v((SMALL, D), F32),
        v((8, D), F32),
        v((1, D), jnp.int32),
        v((2, 1, QB), F32),
        v((OWN, D), BF16),
        v((OWN, D), BF16),
        v((LAYERS, OWN, D), F32),
        v((LAYERS, GROUP, D), BF16),
        v((LAYERS, GROUP, WQ), BF16),
        v((LAYERS, 2, 1, GROUP), F32),
        v((LAYERS, GROUP, OWN), BF16),
        v((LAYERS, OWN, D), F32),
        v((LAYERS, GROUP, D), BF16),
        v((LAYERS, GROUP, WU), F32),
        v((LAYERS, GROUP, WU), BF16),
        v((GROUP, QB), F32),
        v((GROUP, QB), F32),
        v((OWN, GROUP), BF16),
        v((OWN, GROUP), F32),
        v((GROUP, D), BF16),
        v((GROUP, WU), BF16),
        v((GROUP, D), BF16),
        v((GROUP, OWN), BF16),
        v((GROUP, WQ), BF16),
        v((GROUP, OWN), F32),
        v((GROUP, OWN), F32),
        v((7 * OWN, D), BF16),
        v((7 * OWN, D), BF16),
        v((OWN, D), BF16),
        v((OWN, D), F32),
    ]
    copies = 4 * LAYERS * (GATHER_COPIES + SCATTER_COPIES) + 64
    return pl.pallas_call(
        functools.partial(blocks_kernel, y_size),
        out_shape=outs,
        in_specs=in_vmem(2) + [pl.BlockSpec(memory_space=pl.ANY)] * 4 + in_vmem(9),
        out_specs=in_vmem(2) + [pl.BlockSpec(memory_space=pl.ANY if whole else pltpu.VMEM)] * 4 + in_vmem(1),
        scratch_shapes=scratch + [pltpu.SemaphoreType.DMA((copies,)), pltpu.SemaphoreType.DMA((copies,))],
        compiler_params=pltpu.CompilerParams(collective_id=1, has_side_effects=True, vmem_limit_bytes=VMEM_LIMIT),
        cost_estimate=pl.CostEstimate(flops=24 << 30, bytes_accessed=32 << 20, transcendentals=16 << 20),
    )(*args)


ROWS = 32


def unpack_kernel(up, down, qkv, out, small, up_grad, down_grad, qkv_grad, out_grad,
                  g_gain1, g_shift1, g_gain2, g_shift2, g_out_bias, g_down_bias, g_qv_bias, g_up_bias):
    for l in range(LAYERS):
        here = slice(l, l + 1)
        singles = (g_gain1, g_shift1, g_gain2, g_shift2, g_out_bias, g_down_bias)
        for k, ref in enumerate(singles):
            ref[here, :] = small[16 * l + k : 16 * l + k + 1, :]
        for k in range(4):
            g_up_bias[here, k * OWN : (k + 1) * OWN] = small[16 * l + 6 + k : 16 * l + 7 + k, :]
        for k in range(2):
            g_qv_bias[here, k * OWN : (k + 1) * OWN] = small[16 * l + 10 + k : 16 * l + 11 + k, :]
    for w in range(N):
        up_grad[0, :, w * WU : (w + 1) * WU] = up[0, w, 0].astype(F32)
        for part in range(3):
            cols = slice(part * D + w * OWN, part * D + (w + 1) * OWN)
            qkv_grad[0, :, cols] = qkv[0, w, 0, :, part * OWN : (part + 1) * OWN].astype(F32)
    down_grad[0] = down[0].astype(F32)
    out_grad[0] = out[0].astype(F32)


def unpack(up, down, qkv, out, small):
    steps = OWN // ROWS
    per_half = HALF // ROWS

    def pieces(width):
        return pl.BlockSpec((1, N, 1, ROWS, width), lambda l, i: (l, 0, i // per_half, i % per_half, 0))

    def plain(rows, width):
        return pl.BlockSpec((1, rows, width), lambda l, i: (l, i, 0))

    def fixed(rows, width):
        return pl.BlockSpec((rows, width), lambda l, i: (0, 0))

    narrow = [OWN] * 6 + [2 * OWN, WU]
    return pl.pallas_call(
        unpack_kernel,
        grid=(LAYERS, steps),
        in_specs=[pieces(WU), plain(WU // steps, D), pieces(WQ), plain(ROWS, D), fixed(SMALL, OWN)],
        out_specs=[plain(ROWS, FF), plain(WU // steps, D), plain(ROWS, 3 * D), plain(ROWS, D)]
        + [fixed(LAYERS, width) for width in narrow],
        out_shape=[
            struct((LAYERS, OWN, FF), F32),
            struct((LAYERS, WU, D), F32),
            struct((LAYERS, OWN, 3 * D), F32),
            struct((LAYERS, OWN, D), F32),
        ]
        + [struct((LAYERS, width), F32) for width in narrow],
        compiler_params=pltpu.CompilerParams(vmem_limit_bytes=VMEM_LIMIT),
    )(up, down, qkv, out, small)


def per_device(y_size, reduce, tokens, segment_ids, cotangent, gain1, shift1, qkv_weight, qv_bias, out_weight, out_bias,
               gain2, shift2, up_weight, up_bias, down_weight, down_bias):
    output, grad, up, down, qkv, out, small = run_blocks(
        y_size, tokens, cotangent, qkv_weight, up_weight, out_weight, down_weight,
        gain1, shift1, out_bias, gain2, shift2, down_bias, qv_bias, up_bias, segment_ids,
    )
    if reduce is not None:
        up, down, qkv, out, small = reduce(up, down, small)
    up, down, qkv, out, g1, s1, g2, s2, ob, db, qv, ub = unpack(up, down, qkv, out, small)
    return output, grad, g1, s1, qkv, qv, out, ob, g2, s2, up, ub, down, db


def solution(mesh, reduce=None):
    rows = P(None, "shard")
    tiles = P(None, "shard", None)
    tokens = P("replica", "shard", None)
    y_size = 4 if mesh.shape["replica"] == REPLICAS else 1
    return jax.shard_map(
        functools.partial(per_device, y_size, reduce),
        mesh=mesh,
        in_specs=(
            tokens, P("replica", "shard"), tokens,
            rows, rows, tiles, rows, tiles, rows, rows, rows, tiles, rows, tiles, rows,
        ),
        out_specs=(tokens, tokens, rows, rows, tiles, rows, tiles, rows, rows, rows, tiles, rows, tiles, rows),
        check_vma=False,
    )
```
